128 devices in a mesh: section: 4 (over z_lo, core), fsdp: 32 (over x, y, z_hi).
Axes of the slice: x: 4, y: 4, z: 4 (z_hi: 2, z_lo: 2; z = z_hi * 2 + z_lo), core: 2. Of those that a mesh axis runs over, the one named last changes fastest.
Arguments:
- fwd_input: bfloat16 [4, 4096, 6144], P('section', 'fsdp'), may hold values from -6 to 6
- fwd_routes: int32 [4, 4096, 2], P('section', 'fsdp'), may hold values from 0 to 7, all different within a row; in each aligned block of 128 rows (0 to 127, 128 to 255, ..., all dimensions but the last counted through in order) at most 40 rows name the same one
- fwd_weights: float32 [4, 4096, 2], P('section', 'fsdp'), may hold values from 0.25 to 1
- bwd_input: bfloat16 [4, 4096, 6144], P('section', 'fsdp'), may hold values from -6 to 6
- bwd_routes: int32 [4, 4096, 2], P('section', 'fsdp'), may hold values from 0 to 7, all different within a row; in each aligned block of 128 rows (0 to 127, 128 to 255, ..., all dimensions but the last counted through in order) at most 40 rows name the same one
- bwd_weights: float32 [4, 4096, 2], P('section', 'fsdp'), may hold values from 0.25 to 1
- out_grad: bfloat16 [4, 4096, 6144], P('section', 'fsdp'), may hold values from -6 to 6
- up_weight: bfloat16 [4, 6144, 8192], P('section', None, 'fsdp'), may hold values from -0.078125 to 0.078125
- down_weight: bfloat16 [4, 8192, 6144], P('section', 'fsdp'), may hold values from -0.0625 to 0.0625
Outputs:
- next_input: bfloat16 [4, 4096, 6144], P('section', 'fsdp')
- input_grad: bfloat16 [4, 4096, 6144], P('section', 'fsdp')
- up_grad: bfloat16 [4, 6144, 8192], P('section', None, 'fsdp')
- down_grad: bfloat16 [4, 8192, 6144], P('section', 'fsdp')
The draws below stay inside these ranges and needn't reach their ends.
Inputs may be any that keep to these rules, and one draw needn't show every extreme that they name: `fwd_routes`: each row names two different experts. Of the 128 rows of one device and one micro-batch, at most 40 name any one expert; in every draw some device's rows name one expert exactly 40 times. `bwd_routes`: as for fwd_routes.
All inputs are finite; a program needn't handle non-finite values.
Results may differ from the reference program's by a relative error of at most 0.015.
Values may be sent and summed in bfloat16 or wider, within the bound.
A program may use at most 192 MiB of HBM per device.

```python
import math
import jax
import jax.numpy as jnp
import numpy as np
from jax import lax

D = 6144
FF = 8192
EXPERTS = 8
TOK_DEV = 128
CAP = 40
TOKENS = 4096
SECTIONS = 4
N_FSDP = 32


def shard_levels(own_key, shape, cuts, smallest, largest):
    def one(dim, parts):
        steps = jax.random.uniform(jax.random.fold_in(jax.random.fold_in(own_key, 6), dim), (parts,), jnp.float32, smallest / len(cuts), largest / len(cuts))
        return jnp.repeat(jnp.exp(steps), shape[dim] // parts).reshape((-1,) + (1,) * (len(shape) - dim - 1))

    factor_of = one(*cuts[0])
    for cut in cuts[1:]:
        factor_of = factor_of * one(*cut)
    return factor_of


def shared_out(rng, own, number, rows, amount, top, limit, skew):
    ranking = jax.random.permutation(rng, amount)
    crowded, usual = portions_of(amount, rows * top, limit, skew, True), portions_of(amount, rows * top, limit, skew, False)
    places = jnp.arange(amount)

    def named(lengths, rotation):
        used = int((lengths > 0).sum())
        fixed = max(1, used // 4)
        passed = fixed + (places - fixed + rotation * (used - fixed)) % max(1, amount - fixed)
        return jnp.zeros((amount,), jnp.int32).at[ranking[jnp.where(places < fixed, places, passed)]].set(jnp.asarray(lengths, jnp.int32))

    lengths = jnp.where(number % 4 == 0, named(crowded, number // 4), named(usual, number - number // 4 - 1))
    mixed = jax.random.permutation(jax.random.fold_in(own, 3), amount)
    giver, receiver = mixed[0:amount // 2 * 2:2], mixed[1:amount // 2 * 2:2]
    room = jnp.minimum(lengths[giver] - 1, limit - lengths[receiver]) // 2
    room = jnp.where((giver == ranking[0]) | (receiver == ranking[0]) | (lengths[receiver] == 0), 0, jnp.maximum(room, 0))
    passed = jax.random.randint(jax.random.fold_in(own, 4), (amount // 2,), 0, 1 << 20) % (room + 1)
    lengths = lengths.at[giver].add(-passed).at[receiver].add(passed)
    members = jnp.searchsorted(jnp.cumsum(lengths), jnp.arange(rows * top), side="right").astype(jnp.int32)
    listing = members.reshape(top, rows).T
    listing = listing[jax.random.permutation(jax.random.fold_in(own, 1), rows)]
    rotation = jax.random.randint(jax.random.fold_in(own, 2), (rows, 1), 0, top)
    return jnp.take_along_axis(listing, (jnp.arange(top)[None, :] + rotation) % top, axis=1)


def portions_of(number_of, total, limit, skew, full):
    portions = [(1 << 20) // math.isqrt(grade ** skew) + 1 for grade in range(1, number_of + 1)]
    largest = limit if full else min(limit, max(-(-total // number_of), total * portions[0] // sum(portions)))
    least = 1 if total - largest >= number_of - 1 else 0
    given, spare = [largest] + [least] * (number_of - 1), total - largest - least * (number_of - 1)
    while spare > 0:
        free = [i for i in range(1, number_of) if given[i] < largest] or [i for i in range(1, number_of) if given[i] < limit]
        mass, left = sum([portions[i] for i in free]), spare
        for i in free:
            extra = min(limit - given[i], max(1, left * portions[i] // mass), spare)
            given[i] = given[i] + extra
            spare = spare - extra
    return np.array(given)


def bell_draw(key, shape, scale, reach, shards=(), kind=jnp.bfloat16):
    loudness = shard_levels(key, shape, shards, -0.22, 0.18) if shards else 1.0
    array = jax.random.normal(key, shape, jnp.float32) * scale * loudness
    return jnp.minimum(jnp.maximum(array, -reach), reach).astype(kind)


def setup_inputs(seed: int = 0) -> dict:
    arg_keys = jax.random.split(jax.random.key(seed), 10)
    fwd_input = bell_draw(arg_keys[0], (SECTIONS, TOKENS, D), 1.0, 6.0, ((0, 4), (1, 32)))
    fwd_routes_keys = jax.random.split(jax.random.fold_in(arg_keys[1], 1), SECTIONS * TOKENS // TOK_DEV)
    fwd_routes_turns = jax.random.permutation(jax.random.fold_in(arg_keys[1], 3), SECTIONS * TOKENS // TOK_DEV)
    fwd_routes = jax.vmap(lambda own, number: shared_out(jax.random.fold_in(arg_keys[1], 2), own, number, TOK_DEV, EXPERTS, 2, CAP, 2))(fwd_routes_keys, fwd_routes_turns).reshape((SECTIONS, TOKENS, 2))
    fwd_weights = jnp.clip(0.25 + 0.75 * jax.random.uniform(arg_keys[2], (SECTIONS, TOKENS, 2), jnp.float32) ** shard_levels(arg_keys[2], (SECTIONS, TOKENS, 2), ((0, 4), (1, 32)), -0.2, 0.2), 0.25, 1.0)
    bwd_input = bell_draw(arg_keys[3], (SECTIONS, TOKENS, D), 1.0, 6.0, ((0, 4), (1, 32)))
    bwd_routes_keys = jax.random.split(jax.random.fold_in(arg_keys[4], 1), SECTIONS * TOKENS // TOK_DEV)
    bwd_routes_turns = jax.random.permutation(jax.random.fold_in(arg_keys[4], 3), SECTIONS * TOKENS // TOK_DEV)
    bwd_routes = jax.vmap(lambda own, number: shared_out(jax.random.fold_in(arg_keys[4], 2), own, number, TOK_DEV, EXPERTS, 2, CAP, 2))(bwd_routes_keys, bwd_routes_turns).reshape((SECTIONS, TOKENS, 2))
    bwd_weights = jnp.clip(0.25 + 0.75 * jax.random.uniform(arg_keys[5], (SECTIONS, TOKENS, 2), jnp.float32) ** shard_levels(arg_keys[5], (SECTIONS, TOKENS, 2), ((0, 4), (1, 32)), -0.2, 0.2), 0.25, 1.0)
    out_grad = bell_draw(arg_keys[6], (SECTIONS, TOKENS, D), 1.0, 6.0, ((0, 4), (1, 32)))
    up_weight = bell_draw(arg_keys[7], (SECTIONS, D, FF), D ** -0.5, 0.078125, ((0, 4), (2, 32)))
    down_weight = bell_draw(arg_keys[8], (SECTIONS, FF, D), FF ** -0.5, 0.0625, ((0, 4), (1, 32)))
    return dict(fwd_input=fwd_input, fwd_routes=fwd_routes, fwd_weights=fwd_weights, bwd_input=bwd_input, bwd_routes=bwd_routes, bwd_weights=bwd_weights, out_grad=out_grad, up_weight=up_weight, down_weight=down_weight)


def routing_plan(route_ids, route_weights, expert):
    route_ids = route_ids.reshape(N_FSDP, TOK_DEV, 2)
    route_weights = route_weights.reshape(N_FSDP, TOK_DEV, 2)
    matches = route_ids == expert
    active = jnp.any(matches, axis=-1)
    chosen = jnp.sum(jnp.where(matches, route_weights, jnp.float32(0.0)), axis=-1)
    ordinal = jnp.cumsum(active.astype(jnp.int32), axis=-1) - 1
    places = jnp.arange(CAP, dtype=jnp.int32)
    selector = jnp.where((ordinal[:, None, :] == places[None, :, None]) & active[:, None, :], 1.0, 0.0).astype(jnp.float32)
    return selector, chosen.reshape(TOKENS)


def pack_rows(selector, source):
    blocks = source.astype(jnp.float32).reshape(N_FSDP, TOK_DEV, D)
    packed = jnp.einsum("nct,ntd->ncd", selector, blocks, precision=lax.Precision.HIGHEST)
    return packed.reshape(N_FSDP * CAP, D).astype(jnp.bfloat16)


def unpack_rows(selector, packed):
    blocks = packed.reshape(N_FSDP, CAP, D)
    spread = jnp.einsum("nct,ncd->ntd", selector, blocks, precision=lax.Precision.HIGHEST)
    return spread.reshape(TOKENS, D)


def grouped_sum(left, right):
    width = FF // N_FSDP
    count = left.shape[0]
    lefts = left.reshape(count, N_FSDP, width).transpose(1, 0, 2)
    rights = right.reshape(N_FSDP, width, D)

    def add_group(running, pair):
        partial_sum = jnp.dot(pair[0], pair[1], preferred_element_type=jnp.float32)
        rounded = lax.optimization_barrier(partial_sum.astype(jnp.bfloat16))
        return running + rounded.astype(jnp.float32), None

    running, _ = lax.scan(add_group, jnp.zeros((count, D), jnp.float32), (lefts, rights))
    return running


def silu_slope(values):
    sigma = jax.nn.sigmoid(values)
    return sigma * (1.0 + values * (1.0 - sigma))


def reference(fwd_input, fwd_routes, fwd_weights, bwd_input, bwd_routes, bwd_weights, out_grad, up_weight, down_weight):
    section_outs = []
    input_grads = []
    up_grads = []
    down_grads = []
    for which_section in range(SECTIONS):
        upper = up_weight[which_section]
        lower = down_weight[which_section]
        select_f, weight_f = routing_plan(fwd_routes[which_section], fwd_weights[which_section], which_section)
        packed_f = pack_rows(select_f, fwd_input[which_section])
        hidden_f = jax.nn.silu(jnp.dot(packed_f, upper, preferred_element_type=jnp.float32)).astype(jnp.bfloat16)
        expert_f = grouped_sum(hidden_f, lower)
        section_out = fwd_input[which_section].astype(jnp.float32) + weight_f[:, None] * unpack_rows(select_f, expert_f)
        section_outs.append(section_out.astype(jnp.bfloat16))

        select_b, weight_b = routing_plan(bwd_routes[which_section], bwd_weights[which_section], which_section)
        packed_b = pack_rows(select_b, bwd_input[which_section])
        scaled_grad = (weight_b[:, None] * out_grad[which_section].astype(jnp.float32)).astype(jnp.bfloat16)
        packed_g = pack_rows(select_b, scaled_grad)
        pre_b = jnp.dot(packed_b, upper, preferred_element_type=jnp.float32)
        hidden_b = jax.nn.silu(pre_b).astype(jnp.bfloat16)
        down_grads.append(jnp.dot(hidden_b.T, packed_g, preferred_element_type=jnp.float32).astype(jnp.bfloat16))
        back_hidden = jnp.dot(packed_g, lower.T, preferred_element_type=jnp.float32)
        pre_grad = (back_hidden * silu_slope(pre_b)).astype(jnp.bfloat16)
        up_grads.append(jnp.dot(packed_b.T, pre_grad, preferred_element_type=jnp.float32).astype(jnp.bfloat16))
        rows_grad = grouped_sum(pre_grad, upper.T)
        input_grad = out_grad[which_section].astype(jnp.float32) + unpack_rows(select_b, rows_grad)
        input_grads.append(input_grad.astype(jnp.bfloat16))
    next_input = jnp.roll(jnp.stack(section_outs), 1, axis=0)
    return next_input, jnp.stack(input_grads), jnp.stack(up_grads), jnp.stack(down_grads)
```

```python
import functools

import jax
import jax.numpy as jnp
from jax import lax
from jax.experimental import pallas as pl
from jax.experimental.pallas import tpu as pltpu
from jax.sharding import PartitionSpec as P

MESH = pl.DeviceIdType.MESH
F32 = jnp.float32
BF16 = jnp.bfloat16

CAP = 40
SLOTS = 48
D = 6144
HALF = D // 2
UNITS = 256
BLOCK = 2 * CAP
COLS = HALF // 2
QUARTER = COLS // 2
TILE = 768

B, G, F = 0, 1, 2


def kernel(
    pb_ref,
    pg_ref,
    pf_ref,
    up_ref,
    down_ref,
    xf_ref,
    fin_ref,
    fout_ref,
    rout_ref,
    ug_ref,
    dg_ref,
    rows,
    wu,
    wd,
    local,
    remote,
    part,
    peer,
    dgs,
    ugs,
    r1,
    r2,
    r3,
    r4,
    ag_send,
    ag_recv,
    rs_send,
    rs_recv,
    pre_send,
    pre_recv,
    z_send,
    z_recv,
    loc_sem,
):
    sec = lax.axis_index("section")
    me = lax.axis_index("fsdp")
    mx = me // 8
    my = (me // 2) % 4
    zh = me % 2
    mate = me + 1 - 2 * zh
    after = (sec + 1) % 4
    before = (sec + 3) % 4

    def at(x, y):
        return (sec, (((x + 4) % 4) * 4 + (y + 4) % 4) * 2 + zh)

    pair = (sec, mate)

    barrier = pltpu.get_barrier_semaphore()
    near = [
        at(mx + 1, my),
        at(mx - 1, my),
        at(mx, my + 1),
        at(mx, my - 1),
        pair,
        (after, me),
        (after, mate),
        (before, me),
        (before, mate),
    ]
    for device in near:
        pl.semaphore_signal(barrier, inc=1, device_id=device, device_id_type=MESH)
    pl.semaphore_wait(barrier, len(near))

    mine = pl.ds(pl.multiple_of(zh * HALF, HALF), HALF)
    other = pl.ds(pl.multiple_of((1 - zh) * HALF, HALF), HALF)
    started = []

    def send(src, dst, send_sem, recv_sem, device):
        copy = pltpu.make_async_remote_copy(
            src_ref=src,
            dst_ref=dst,
            send_sem=send_sem,
            recv_sem=recv_sem,
            device_id=device,
            device_id_type=MESH,
        )
        copy.start()
        return copy

    def keep(src, dst, index):
        copy = pltpu.make_async_copy(src, dst, loc_sem.at[index])
        copy.start()
        return copy

    def zsend(src, dst, index, device=pair):
        return send(src, dst, z_send.at[index], z_recv.at[index], device)

    packed = (pb_ref, pg_ref, pf_ref)
    token = [zsend(packed[s].at[:, other], remote.at[s], s) for s in (B, G, F)]
    own = [keep(packed[s].at[:, mine], local.at[s], s) for s in (B, G, F)]
    wu_in = zsend(up_ref.at[other], wu.at[1], 3)
    wu_own = keep(up_ref.at[mine], wu.at[0], 3)
    wd_own = keep(down_ref.at[:, mine], wd.at[0], 4)

    slot = lax.broadcasted_iota(jnp.int32, (BLOCK, SLOTS), 1)
    row = lax.broadcasted_iota(jnp.int32, (BLOCK, SLOTS), 0)

    def place(which):
        hit = (row == slot + CAP * which) & (slot < CAP)
        return jnp.where(hit, 1.0, 0.0).astype(BF16)

    place_mine, place_other = place(zh), place(1 - zh)

    def fill(s):
        token[s].wait_recv()
        own[s].wait()
        for c in range(0, HALF, TILE):
            cols = pl.ds(c, TILE)
            total = jnp.dot(place_mine, local[s, :, cols], preferred_element_type=F32)
            total += jnp.dot(place_other, remote[s, :, cols], preferred_element_type=F32)
            rows[s, mx, my, :, cols] = total.astype(BF16)

    def up4(i):
        return (i + 4) % 4

    def one(h, i):
        return (up4(i), my) if h == 0 else (mx, up4(i))

    def g1(s, h, i, start, width):
        x, y = one(h, i)
        return rows.at[s, x, y, :, pl.ds(h * COLS + start, width)]

    def g4(s, h, j, start, width):
        cols = pl.ds(h * COLS + start, width)
        if h == 0:
            return rows.at[s, :, up4(j), :, cols]
        return rows.at[s, up4(j), :, :, cols]

    first, second = (mx, my), (my, mx)

    def dev1(h, step):
        return at(mx + step, my) if h == 0 else at(mx, my + step)

    def dev2(h, step):
        return at(mx, my + step) if h == 0 else at(mx + step, my)

    gathers = {}

    def gsend(s, h, k, ref, device):
        gathers[s, h, k] = send(ref, ref, ag_send.at[s, h, k], ag_recv.at[s, h, k], device)

    def gather1(s):
        for h in (0, 1):
            ref = g1(s, h, first[h], 0, COLS)
            gsend(s, h, 0, ref, dev1(h, 1))
            gsend(s, h, 1, ref, dev1(h, -1))

    def gather2(s):
        for h in (0, 1):
            gathers[s, h, 0].wait_recv()
            gsend(s, h, 2, g1(s, h, first[h] - 1, 0, QUARTER), dev1(h, 1))
            gathers[s, h, 1].wait_recv()
            gsend(s, h, 3, g1(s, h, first[h] + 1, QUARTER, QUARTER), dev1(h, -1))

    def gather3(s):
        for h in (0, 1):
            gathers[s, h, 2].wait_recv()
            gathers[s, h, 3].wait_recv()
            ref = g4(s, h, second[h], 0, COLS)
            gsend(s, h, 4, ref, dev2(h, 1))
            gsend(s, h, 5, ref, dev2(h, -1))

    def gather4(s):
        for h in (0, 1):
            gathers[s, h, 4].wait_recv()
            gsend(s, h, 6, g4(s, h, second[h] - 1, 0, QUARTER), dev2(h, 1))
            gathers[s, h, 5].wait_recv()
            gsend(s, h, 7, g4(s, h, second[h] + 1, QUARTER, QUARTER), dev2(h, -1))

    def gather5(s):
        for h in (0, 1):
            gathers[s, h, 6].wait_recv()
            gathers[s, h, 7].wait_recv()

    def gathered_out(s):
        for h in (0, 1):
            for k in range(8):
                gathers[s, h, k].wait_send()

    def pre_copy(s, i):
        return pltpu.make_async_remote_copy(
            src_ref=part.at[s, i],
            dst_ref=peer.at[s, i],
            send_sem=pre_send.at[s, i],
            recv_sem=pre_recv.at[s, i],
            device_id=pair,
            device_id_type=MESH,
        )

    last = (((1,), (1,)), ((), ()))
    lead = (((0,), (0,)), ((), ()))

    def partial_up(s):
        def step(i, carry):
            block = rows[s, i].reshape(4 * BLOCK, HALF)
            for u in (0, 1):
                value = jnp.dot(block, wu[u], preferred_element_type=F32)
                part[s, i, :, pl.ds(u * UNITS, UNITS)] = value.astype(BF16)
            pre_copy(s, i).start()
            return carry

        lax.fori_loop(0, 4, step, 0)

    def partial_back(s):
        def step(i, carry):
            block = rows[s, i].reshape(4 * BLOCK, HALF)
            for u in (0, 1):
                value = lax.dot_general(block, wd[u], last, preferred_element_type=F32)
                part[s, i, :, pl.ds(u * UNITS, UNITS)] = value.astype(BF16)
            pre_copy(s, i).start()
            return carry

        lax.fori_loop(0, 4, step, 0)

    def whole(s, i, u):
        here = part[s, i, :, pl.ds(u * UNITS, UNITS)].astype(F32)
        return here + peer[s, i, :, pl.ds((1 - u) * UNITS, UNITS)].astype(F32)

    def sigmoid(value):
        return 1.0 / (1.0 + jnp.exp(-value))

    def activate_back():
        def step(i, carry):
            pre_copy(B, i).wait_recv()
            pre_copy(G, i).wait_recv()
            hidden, slope = [], []
            for u in (0, 1):
                pre = whole(B, i, u)
                gate = sigmoid(pre)
                hidden.append((pre * gate).astype(BF16))
                back = whole(G, i, u)
                slope.append((back * (gate * (1.0 + pre * (1.0 - gate)))).astype(BF16))
            for u in (0, 1):
                peer[B, i, :, pl.ds(u * UNITS, UNITS)] = hidden[u]
                peer[G, i, :, pl.ds(u * UNITS, UNITS)] = slope[u]
            return carry

        lax.fori_loop(0, 4, step, 0)

    def activate_fwd():
        def step(i, carry):
            pre_copy(F, i).wait_recv()
            hidden = []
            for u in (0, 1):
                pre = whole(F, i, u)
                hidden.append((pre * sigmoid(pre)).astype(BF16))
            for u in (0, 1):
                peer[F, i, :, pl.ds(u * UNITS, UNITS)] = hidden[u]
            return carry

        lax.fori_loop(0, 4, step, 0)

    def down_grad():
        for u in (1, 0):
            def step(c, carry):
                cols = pl.ds(pl.multiple_of(c * TILE, TILE), TILE)
                left = peer[B, :, :, pl.ds(u * UNITS, UNITS)].reshape(16 * BLOCK, UNITS)
                right = rows[G, :, :, :, cols].reshape(16 * BLOCK, TILE)
                value = lax.dot_general(left, right, lead, preferred_element_type=F32)
                dgs[u, :, cols] = value.astype(BF16)
                return carry

            lax.fori_loop(0, HALF // TILE, step, 0)

    def up_grad():
        def step(c, carry):
            cols = pl.ds(pl.multiple_of(c * TILE, TILE), TILE)
            left = rows[B, :, :, :, cols].reshape(16 * BLOCK, TILE)
            for u in (0, 1):
                right = peer[G, :, :, pl.ds(u * UNITS, UNITS)].reshape(16 * BLOCK, UNITS)
                value = lax.dot_general(left, right, lead, preferred_element_type=F32)
                ugs[u, cols, :] = value.astype(BF16)
            return carry

        lax.fori_loop(0, HALF // TILE, step, 0)

    def rows_out(s, source, weights, dims):
        def step(n, carry):
            i = n // (HALF // TILE)
            c = n % (HALF // TILE)
            cols = pl.ds(pl.multiple_of(c * TILE, TILE), TILE)
            total = None
            for u in (0, 1):
                left = peer[source, i, :, pl.ds(u * UNITS, UNITS)]
                right = weights[u, cols, :] if dims == last else weights[u, :, cols]
                if dims == last:
                    value = lax.dot_general(left, right, last, preferred_element_type=F32)
                else:
                    value = jnp.dot(left, right, preferred_element_type=F32)
                total = value if total is None else total + value
            rows[s, i, :, :, cols] = total.astype(BF16).reshape(4, BLOCK, TILE)
            return carry

        lax.fori_loop(0, 4 * (HALF // TILE), step, 0)

    scatters = {}

    def ssend(s, h, k, src, dst, device):
        scatters[s, h, k] = send(src, dst, rs_send.at[s - 1, h, k], rs_recv.at[s - 1, h, k], device)

    def add4(s, h, j, start, width, sources):
        cols = pl.ds(h * COLS + start, width)

        def step(i, carry):
            x, y = (i, up4(j)) if h == 0 else (up4(j), i)
            total = rows[s, x, y, :, cols].astype(F32)
            for source in sources:
                total += source[i].astype(F32)
            rows[s, x, y, :, cols] = total.astype(BF16)
            return carry

        lax.fori_loop(0, 4, step, 0)

    def sum1(s, h, i, start, width, sources):
        x, y = one(h, i)
        total = rows[s, x, y, :, pl.ds(h * COLS + start, width)].astype(F32)
        for source in sources:
            total += source[...].astype(F32)
        rows[s, x, y, :, pl.ds(h * COLS + start, width)] = total.astype(BF16)

    def scatter1(s):
        for h in (0, 1):
            far = second[h] + 2
            ssend(s, h, 0, g4(s, h, far, 0, QUARTER), r1.at[s - 1, h, 0], dev2(h, 1))
            ssend(s, h, 1, g4(s, h, far, QUARTER, QUARTER), r1.at[s - 1, h, 1], dev2(h, -1))

    def scatter2(s):
        for h in (0, 1):
            scatters[s, h, 0].wait_recv()
            add4(s, h, second[h] + 1, 0, QUARTER, [r1.at[s - 1, h, 0]])
            ssend(s, h, 2, g4(s, h, second[h] + 1, 0, COLS), r2.at[s - 1, h, 0], dev2(h, 1))
            scatters[s, h, 1].wait_recv()
            add4(s, h, second[h] - 1, QUARTER, QUARTER, [r1.at[s - 1, h, 1]])
            ssend(s, h, 3, g4(s, h, second[h] - 1, 0, COLS), r2.at[s - 1, h, 1], dev2(h, -1))

    def scatter3(s):
        for h in (0, 1):
            scatters[s, h, 2].wait_recv()
            scatters[s, h, 3].wait_recv()
            add4(s, h, second[h], 0, COLS, [r2.at[s - 1, h, 0], r2.at[s - 1, h, 1]])
            far = first[h] + 2
            ssend(s, h, 4, g1(s, h, far, 0, QUARTER), r3.at[s - 1, h, 0], dev1(h, 1))
            ssend(s, h, 5, g1(s, h, far, QUARTER, QUARTER), r3.at[s - 1, h, 1], dev1(h, -1))

    def scatter4(s):
        for h in (0, 1):
            scatters[s, h, 4].wait_recv()
            sum1(s, h, first[h] + 1, 0, QUARTER, [r3.at[s - 1, h, 0]])
            ssend(s, h, 6, g1(s, h, first[h] + 1, 0, COLS), r4.at[s - 1, h, 0], dev1(h, 1))
            scatters[s, h, 5].wait_recv()
            sum1(s, h, first[h] - 1, QUARTER, QUARTER, [r3.at[s - 1, h, 1]])
            ssend(s, h, 7, g1(s, h, first[h] - 1, 0, COLS), r4.at[s - 1, h, 1], dev1(h, -1))

    def scatter5(s, mine_ref, other_ref):
        for h in (0, 1):
            scatters[s, h, 6].wait_recv()
            scatters[s, h, 7].wait_recv()
            sum1(s, h, first[h], 0, COLS, [r4.at[s - 1, h, 0], r4.at[s - 1, h, 1]])
        for c in range(0, HALF, TILE):
            cols = pl.ds(c, TILE)
            block = rows[s, mx, my, :, cols]
            mine_ref[:, cols] = lax.dot_general(
                place_mine, block, lead, preferred_element_type=F32
            ).astype(BF16)
            other_ref[:, cols] = lax.dot_general(
                place_other, block, lead, preferred_element_type=F32
            ).astype(BF16)

    fill(B)
    gather1(B)
    gather2(B)
    gather3(B)
    wd_in = zsend(down_ref.at[:, other], wd.at[1], 4)
    fill(G)
    gather1(G)
    gather2(G)
    gather4(B)
    gather3(G)
    fill(F)
    gather1(F)
    gather5(B)
    wu_in.wait_recv()
    wu_own.wait()
    partial_up(B)
    gather4(G)
    gather2(F)
    gather3(F)
    fin = zsend(xf_ref, fin_ref, 10, (after, me))
    gather5(G)
    wd_in.wait_recv()
    wd_own.wait()
    partial_back(G)
    gather4(F)
    gather5(F)
    partial_up(F)
    activate_back()
    down_grad()
    dg_out = zsend(dgs.at[1], dg_ref.at[:, mine], 5)
    dg_own = keep(dgs.at[0], dg_ref.at[:, mine], 5)
    gathered_out(G)
    rows_out(G, G, wu, last)
    scatter1(G)
    up_grad()
    ug_out = zsend(ugs.at[1], ug_ref.at[mine], 6)
    ug_own = keep(ugs.at[0], ug_ref.at[mine], 6)
    scatter2(G)
    activate_fwd()
    gathered_out(F)
    rows_out(F, F, wd, None)
    scatter1(F)
    scatter3(G)
    scatter2(F)
    scatter4(G)
    scatter3(F)
    token[B].wait_send()
    token[G].wait_send()
    token[F].wait_send()
    scatter5(G, local.at[0], local.at[1])
    row_own = keep(local.at[0], rout_ref.at[zh], 7)
    row_out = zsend(local.at[1], rout_ref.at[zh], 7)
    scatter4(F)
    scatter5(F, local.at[2], remote.at[0])
    near_out = zsend(local.at[2], fout_ref.at[zh], 8, (after, me))
    far_out = zsend(remote.at[0], fout_ref.at[zh], 9, (after, mate))

    for copy in (dg_own, ug_own, row_own):
        copy.wait()
    for copy in (dg_out, ug_out, row_out, near_out, far_out, fin):
        copy.wait()
    wu_in.wait_send()
    wd_in.wait_send()
    gathered_out(B)
    for s in (G, F):
        for h in (0, 1):
            for k in range(8):
                scatters[s, h, k].wait_send()

    def done(n, carry):
        pre_copy(n // 4, n % 4).wait_send()
        return carry

    lax.fori_loop(0, 12, done, 0)


def relay(pb, pg, pf, upper, lower, rows):
    hbm = pl.BlockSpec(memory_space=pl.ANY)
    shapes = [
        jax.ShapeDtypeStruct(rows.shape, BF16),
        jax.ShapeDtypeStruct((2, SLOTS, HALF), BF16),
        jax.ShapeDtypeStruct((2, SLOTS, HALF), BF16),
        jax.ShapeDtypeStruct(upper.shape, BF16),
        jax.ShapeDtypeStruct(lower.shape, BF16),
    ]
    dma = pltpu.SemaphoreType.DMA
    return pl.pallas_call(
        kernel,
        out_shape=shapes,
        in_specs=[hbm] * 6,
        out_specs=[hbm] * 5,
        scratch_shapes=[
            pltpu.VMEM((3, 4, 4, BLOCK, HALF), BF16),
            pltpu.VMEM((2, HALF, UNITS), BF16),
            pltpu.VMEM((2, UNITS, HALF), BF16),
            pltpu.VMEM((3, SLOTS, HALF), BF16),
            pltpu.VMEM((3, SLOTS, HALF), BF16),
            pltpu.VMEM((3, 4, 4 * BLOCK, 2 * UNITS), BF16),
            pltpu.VMEM((3, 4, 4 * BLOCK, 2 * UNITS), BF16),
            pltpu.VMEM((2, UNITS, HALF), BF16),
            pltpu.VMEM((2, HALF, UNITS), BF16),
            pltpu.VMEM((2, 2, 2, 4, BLOCK, QUARTER), BF16),
            pltpu.VMEM((2, 2, 2, 4, BLOCK, COLS), BF16),
            pltpu.VMEM((2, 2, 2, BLOCK, QUARTER), BF16),
            pltpu.VMEM((2, 2, 2, BLOCK, COLS), BF16),
            dma((3, 2, 8)),
            dma((3, 2, 8)),
            dma((2, 2, 8)),
            dma((2, 2, 8)),
            dma((3, 4)),
            dma((3, 4)),
            dma((11,)),
            dma((11,)),
            dma((8,)),
        ],
        compiler_params=pltpu.CompilerParams(
            collective_id=0, has_side_effects=True, vmem_limit_bytes=64 * 1024 * 1024
        ),
        cost_estimate=pl.CostEstimate(
            flops=28_000_000_000, bytes_accessed=40_000_000, transcendentals=2_000_000
        ),
        name="relay",
    )(pb, pg, pf, upper, lower, rows)


def from_behind(value, axis, steps):
    count = lax.axis_size(axis)
    pairs = [(source, (source + steps) % count) for source in range(count)]
    return lax.ppermute(value, axis, pairs)


def routing_plan(route_ids, route_weights, expert):
    matches = route_ids == expert
    active = jnp.any(matches, axis=-1)
    chosen = jnp.sum(jnp.where(matches, route_weights, jnp.float32(0.0)), axis=-1)
    ordinal = jnp.cumsum(active.astype(jnp.int32)) - 1
    places = jnp.arange(SLOTS, dtype=jnp.int32)
    hit = (ordinal[None, :] == places[:, None]) & active[None, :]
    return jnp.where(hit, 1.0, 0.0).astype(BF16), chosen


def pack_rows(selector, source):
    return jnp.dot(selector, source, preferred_element_type=F32).astype(BF16)


def unpack_rows(selector, packed):
    halves = [jnp.dot(selector.T, packed[h], preferred_element_type=F32) for h in (0, 1)]
    return jnp.concatenate(halves, axis=1)


def body(
    fwd_input,
    fwd_routes,
    fwd_weights,
    bwd_input,
    bwd_routes,
    bwd_weights,
    out_grad,
    up_weight,
    down_weight,
):
    expert = lax.axis_index("section")
    incoming = out_grad[0]
    select_b, weight_b = routing_plan(bwd_routes[0], bwd_weights[0], expert)
    packed_b = pack_rows(select_b, bwd_input[0])
    scaled_grad = (weight_b[:, None] * incoming.astype(F32)).astype(BF16)
    packed_g = pack_rows(select_b, scaled_grad)
    select_f, _ = routing_plan(fwd_routes[0], fwd_weights[0], expert)
    packed_f = pack_rows(select_f, fwd_input[0])
    routes_p = from_behind(fwd_routes[0], "section", 1)
    weights_p = from_behind(fwd_weights[0], "section", 1)
    rows_p, expert_p, rows_grad, up_grad, down_grad = relay(
        packed_b, packed_g, packed_f, up_weight[0], down_weight[0], fwd_input[0]
    )
    select_p, weight_p = routing_plan(routes_p, weights_p, (expert + 3) % 4)
    next_input = rows_p.astype(F32) + weight_p[:, None] * unpack_rows(select_p, expert_p)
    input_grad = incoming.astype(F32) + unpack_rows(select_b, rows_grad)
    return (
        next_input.astype(BF16)[None],
        input_grad.astype(BF16)[None],
        up_grad[None],
        down_grad[None],
    )


def solution(mesh):
    row_spec = P("section", "fsdp", None)
    in_specs = (row_spec,) * 7 + (P("section", None, "fsdp"), row_spec)
    out_specs = (row_spec, row_spec, P("section", None, "fsdp"), row_spec)
    return jax.shard_map(body, mesh=mesh, in_specs=in_specs, out_specs=out_specs, check_vma=False)
```

```python
import functools

import jax
import jax.numpy as jnp
from jax import lax
from jax.experimental import pallas as pl
from jax.experimental.pallas import tpu as pltpu
from jax.sharding import PartitionSpec as P

MESH = pl.DeviceIdType.MESH
F32 = jnp.float32
BF16 = jnp.bfloat16

CAP = 40
SLOTS = 48
D = 6144
HALF = D // 2
UNITS = 256
TOKENS = 128
BLOCK = 2 * CAP
COLS = HALF // 2
QUARTER = COLS // 2
TILE = 768

B, G, F = 0, 1, 2


def route(plan_ref, base, expert):
    hit = [plan_ref[pl.ds(base + k, 1), :] == expert for k in (0, 1)]
    share = [plan_ref[pl.ds(base + 2 + k, 1), :] for k in (0, 1)]
    active = jnp.where(hit[0] | hit[1], 1.0, 0.0)
    weight = jnp.where(hit[0], share[0], 0.0) + jnp.where(hit[1], share[1], 0.0)
    earlier = lax.broadcasted_iota(jnp.int32, (TOKENS, TOKENS), 0)
    later = lax.broadcasted_iota(jnp.int32, (TOKENS, TOKENS), 1)
    before = jnp.where(earlier < later, 1.0, 0.0).astype(BF16)
    spread = jnp.broadcast_to(active, (8, TOKENS)).astype(BF16)
    order = jnp.dot(spread, before, preferred_element_type=F32)[0:1]
    return order, active, weight


def kernel(
    plan_ref,
    xb_ref,
    xg_ref,
    xf_ref,
    up_ref,
    down_ref,
    fin_ref,
    fout_ref,
    rout_ref,
    ug_ref,
    dg_ref,
    info_ref,
    info,
    rows,
    wu,
    wd,
    local,
    remote,
    part,
    peer,
    dgs,
    ugs,
    r1,
    r2,
    r3,
    r4,
    ag_send,
    ag_recv,
    rs_send,
    rs_recv,
    pre_send,
    pre_recv,
    z_send,
    z_recv,
    loc_sem,
):
    sec = lax.axis_index("section")
    me = lax.axis_index("fsdp")
    mx = me // 8
    my = (me // 2) % 4
    zh = me % 2
    mate = me + 1 - 2 * zh
    after = (sec + 1) % 4
    before = (sec + 3) % 4

    def at(x, y):
        return (sec, (((x + 4) % 4) * 4 + (y + 4) % 4) * 2 + zh)

    pair = (sec, mate)

    barrier = pltpu.get_barrier_semaphore()
    near = [
        at(mx + 1, my),
        at(mx - 1, my),
        at(mx, my + 1),
        at(mx, my - 1),
        pair,
        (after, me),
        (after, mate),
        (before, me),
        (before, mate),
    ]
    for device in near:
        pl.semaphore_signal(barrier, inc=1, device_id=device, device_id_type=MESH)
    pl.semaphore_wait(barrier, len(near))

    mine = pl.ds(pl.multiple_of(zh * HALF, HALF), HALF)
    other = pl.ds(pl.multiple_of((1 - zh) * HALF, HALF), HALF)
    started = []

    def send(src, dst, send_sem, recv_sem, device):
        copy = pltpu.make_async_remote_copy(
            src_ref=src,
            dst_ref=dst,
            send_sem=send_sem,
            recv_sem=recv_sem,
            device_id=device,
            device_id_type=MESH,
        )
        copy.start()
        return copy

    def keep(src, dst, index):
        copy = pltpu.make_async_copy(src, dst, loc_sem.at[index])
        copy.start()
        return copy

    def zsend(src, dst, index, device=pair):
        return send(src, dst, z_send.at[index], z_recv.at[index], device)

    def up_part(n):
        width = HALF // 4
        start = pl.multiple_of((1 - zh) * HALF + n * width, width)
        return zsend(up_ref.at[pl.ds(start, width)], wu.at[1, pl.ds(n * width, width)], 11 + n)

    wu_in = [up_part(0)]
    upper, lower = pl.ds(0, TOKENS), pl.ds(TOKENS, TOKENS)

    def fetch(source, where, index):
        return [
            keep(source.at[:, pl.ds(half * HALF, HALF)], dgs.at[half, where], index + half)
            for half in (0, 1)
        ]

    fetched = {B: fetch(xb_ref, upper, 0), G: fetch(xg_ref, lower, 2)}

    def selector(order, active, count, offset):
        place = lax.broadcasted_iota(jnp.int32, (count, TOKENS), 0).astype(F32)
        return jnp.where((order + offset == place) & (active > 0.0), 1.0, 0.0)

    expert = sec.astype(F32)
    order_b, active_b, weight_b = route(plan_ref, 4, expert)
    order_f, active_f, weight_f = route(plan_ref, 0, expert)
    shift = (CAP * zh).astype(F32)
    line = lax.broadcasted_iota(jnp.int32, (8, TOKENS), 0)
    slots_f = jnp.where(active_f > 0.0, order_f, -1.0)
    info[...] = jnp.where(line == 0, slots_f, jnp.where(line == 1, weight_f, 0.0))

    slot = lax.broadcasted_iota(jnp.int32, (BLOCK, SLOTS), 1)
    row = lax.broadcasted_iota(jnp.int32, (BLOCK, SLOTS), 0)

    def place(which):
        hit = (row == slot + CAP * which) & (slot < CAP)
        return jnp.where(hit, 1.0, 0.0).astype(BF16)

    place_mine, place_other = place(zh), place(1 - zh)

    def pack(s, where, order, active, weight):
        for copy in fetched[s]:
            copy.wait()
        small = selector(order, active, SLOTS, 0.0)
        wide = selector(order, active, BLOCK, shift)
        small_w = jnp.sum(small * weight, axis=1, keepdims=True)
        wide_w = jnp.sum(wide * weight, axis=1, keepdims=True)
        for c in range(0, HALF, TILE):
            cols = pl.ds(c, TILE)
            value = jnp.dot(small.astype(BF16), dgs[1 - zh, where, cols], preferred_element_type=F32)
            if s == G:
                value = value * small_w
            local[s, :, cols] = value.astype(BF16)
        copy = zsend(local.at[s], remote.at[s], s)
        for c in range(0, HALF, TILE):
            cols = pl.ds(c, TILE)
            value = jnp.dot(wide.astype(BF16), dgs[zh, where, cols], preferred_element_type=F32)
            if s == G:
                value = value * wide_w
            rows[s, mx, my, :, cols] = value.astype(BF16)
        return copy

    token = {}

    def fill(s):
        token[s].wait_recv()
        for c in range(0, HALF, TILE):
            cols = pl.ds(c, TILE)
            total = jnp.dot(place_other, remote[s, :, cols], preferred_element_type=F32)
            total += rows[s, mx, my, :, cols].astype(F32)
            rows[s, mx, my, :, cols] = total.astype(BF16)

    def up4(i):
        return (i + 4) % 4

    def one(h, i):
        return (up4(i), my) if h == 0 else (mx, up4(i))

    def g1(s, h, i, start, width):
        x, y = one(h, i)
        return rows.at[s, x, y, :, pl.ds(h * COLS + start, width)]

    def g4(s, h, j, start, width):
        cols = pl.ds(h * COLS + start, width)
        if h == 0:
            return rows.at[s, :, up4(j), :, cols]
        return rows.at[s, up4(j), :, :, cols]

    first, second = (mx, my), (my, mx)

    def dev1(h, step):
        return at(mx + step, my) if h == 0 else at(mx, my + step)

    def dev2(h, step):
        return at(mx, my + step) if h == 0 else at(mx + step, my)

    gathers = {}

    def gsend(s, h, k, ref, device):
        gathers[s, h, k] = send(ref, ref, ag_send.at[s, h, k], ag_recv.at[s, h, k], device)

    def gather1(s):
        for h in (0, 1):
            ref = g1(s, h, first[h], 0, COLS)
            gsend(s, h, 0, ref, dev1(h, 1))
            gsend(s, h, 1, ref, dev1(h, -1))

    def gather2(s):
        for h in (0, 1):
            gathers[s, h, 0].wait_recv()
            gsend(s, h, 2, g1(s, h, first[h] - 1, 0, QUARTER), dev1(h, 1))
            gathers[s, h, 1].wait_recv()
            gsend(s, h, 3, g1(s, h, first[h] + 1, QUARTER, QUARTER), dev1(h, -1))

    def gather3(s):
        for h in (0, 1):
            gathers[s, h, 2].wait_recv()
            gathers[s, h, 3].wait_recv()
            ref = g4(s, h, second[h], 0, COLS)
            gsend(s, h, 4, ref, dev2(h, 1))
            gsend(s, h, 5, ref, dev2(h, -1))

    def gather4(s):
        for h in (0, 1):
            gathers[s, h, 4].wait_recv()
            gsend(s, h, 6, g4(s, h, second[h] - 1, 0, QUARTER), dev2(h, 1))
            gathers[s, h, 5].wait_recv()
            gsend(s, h, 7, g4(s, h, second[h] + 1, QUARTER, QUARTER), dev2(h, -1))

    def gather5(s):
        for h in (0, 1):
            gathers[s, h, 6].wait_recv()
            gathers[s, h, 7].wait_recv()

    def gathered_out(s):
        for h in (0, 1):
            for k in range(8):
                gathers[s, h, k].wait_send()

    def pre_copy(s, i):
        return pltpu.make_async_remote_copy(
            src_ref=part.at[s, i],
            dst_ref=peer.at[s, i],
            send_sem=pre_send.at[s, i],
            recv_sem=pre_recv.at[s, i],
            device_id=pair,
            device_id_type=MESH,
        )

    last = (((1,), (1,)), ((), ()))
    lead = (((0,), (0,)), ((), ()))

    def partial_up(s):
        def step(i, carry):
            block = rows[s, i].reshape(4 * BLOCK, HALF)
            for u in (0, 1):
                value = jnp.dot(block, wu[u], preferred_element_type=F32)
                part[s, i, :, pl.ds(u * UNITS, UNITS)] = value.astype(BF16)
            pre_copy(s, i).start()
            return carry

        lax.fori_loop(0, 4, step, 0)

    def partial_back(s):
        def step(i, carry):
            block = rows[s, i].reshape(4 * BLOCK, HALF)
            for u in (0, 1):
                value = lax.dot_general(block, wd[u], last, preferred_element_type=F32)
                part[s, i, :, pl.ds(u * UNITS, UNITS)] = value.astype(BF16)
            pre_copy(s, i).start()
            return carry

        lax.fori_loop(0, 4, step, 0)

    def whole(s, i, u):
        here = part[s, i, :, pl.ds(u * UNITS, UNITS)].astype(F32)
        return here + peer[s, i, :, pl.ds((1 - u) * UNITS, UNITS)].astype(F32)

    def sigmoid(value):
        return 1.0 / (1.0 + jnp.exp(-value))

    def activate_back():
        def step(i, carry):
            pre_copy(B, i).wait_recv()
            pre_copy(G, i).wait_recv()
            hidden, slope = [], []
            for u in (0, 1):
                pre = whole(B, i, u)
                gate = sigmoid(pre)
                hidden.append((pre * gate).astype(BF16))
                back = whole(G, i, u)
                slope.append((back * (gate * (1.0 + pre * (1.0 - gate)))).astype(BF16))
            for u in (0, 1):
                peer[B, i, :, pl.ds(u * UNITS, UNITS)] = hidden[u]
                peer[G, i, :, pl.ds(u * UNITS, UNITS)] = slope[u]
            return carry

        lax.fori_loop(0, 4, step, 0)

    def activate_fwd():
        def step(i, carry):
            pre_copy(F, i).wait_recv()
            hidden = []
            for u in (0, 1):
                pre = whole(F, i, u)
                hidden.append((pre * sigmoid(pre)).astype(BF16))
            for u in (0, 1):
                peer[F, i, :, pl.ds(u * UNITS, UNITS)] = hidden[u]
            return carry

        lax.fori_loop(0, 4, step, 0)

    def down_grad():
        for u in (1, 0):
            def step(c, carry):
                cols = pl.ds(pl.multiple_of(c * TILE, TILE), TILE)
                left = peer[B, :, :, pl.ds(u * UNITS, UNITS)].reshape(16 * BLOCK, UNITS)
                right = rows[G, :, :, :, cols].reshape(16 * BLOCK, TILE)
                value = lax.dot_general(left, right, lead, preferred_element_type=F32)
                dgs[u, :, cols] = value.astype(BF16)
                return carry

            lax.fori_loop(0, HALF // TILE, step, 0)

    def up_grad():
        def step(c, carry):
            cols = pl.ds(pl.multiple_of(c * TILE, TILE), TILE)
            left = rows[B, :, :, :, cols].reshape(16 * BLOCK, TILE)
            for u in (0, 1):
                right = peer[G, :, :, pl.ds(u * UNITS, UNITS)].reshape(16 * BLOCK, UNITS)
                value = lax.dot_general(left, right, lead, preferred_element_type=F32)
                ugs[u, cols, :] = value.astype(BF16)
            return carry

        lax.fori_loop(0, HALF // TILE, step, 0)

    def rows_out(s, source, weights, dims):
        def step(n, carry):
            i = n // (HALF // TILE)
            c = n % (HALF // TILE)
            cols = pl.ds(pl.multiple_of(c * TILE, TILE), TILE)
            total = None
            for u in (0, 1):
                left = peer[source, i, :, pl.ds(u * UNITS, UNITS)]
                right = weights[u, cols, :] if dims == last else weights[u, :, cols]
                if dims == last:
                    value = lax.dot_general(left, right, last, preferred_element_type=F32)
                else:
                    value = jnp.dot(left, right, preferred_element_type=F32)
                total = value if total is None else total + value
            rows[s, i, :, :, cols] = total.astype(BF16).reshape(4, BLOCK, TILE)
            return carry

        lax.fori_loop(0, 4 * (HALF // TILE), step, 0)

    scatters = {}

    def ssend(s, h, k, src, dst, device):
        scatters[s, h, k] = send(src, dst, rs_send.at[s - 1, h, k], rs_recv.at[s - 1, h, k], device)

    def add4(s, h, j, start, width, sources):
        cols = pl.ds(h * COLS + start, width)

        def step(i, carry):
            x, y = (i, up4(j)) if h == 0 else (up4(j), i)
            total = rows[s, x, y, :, cols].astype(F32)
            for source in sources:
                total += source[i].astype(F32)
            rows[s, x, y, :, cols] = total.astype(BF16)
            return carry

        lax.fori_loop(0, 4, step, 0)

    def sum1(s, h, i, start, width, sources):
        x, y = one(h, i)
        total = rows[s, x, y, :, pl.ds(h * COLS + start, width)].astype(F32)
        for source in sources:
            total += source[...].astype(F32)
        rows[s, x, y, :, pl.ds(h * COLS + start, width)] = total.astype(BF16)

    def scatter1(s):
        for h in (0, 1):
            far = second[h] + 2
            ssend(s, h, 0, g4(s, h, far, 0, QUARTER), r1.at[s - 1, h, 0], dev2(h, 1))
            ssend(s, h, 1, g4(s, h, far, QUARTER, QUARTER), r1.at[s - 1, h, 1], dev2(h, -1))

    def scatter2(s):
        for h in (0, 1):
            scatters[s, h, 0].wait_recv()
            add4(s, h, second[h] + 1, 0, QUARTER, [r1.at[s - 1, h, 0]])
            ssend(s, h, 2, g4(s, h, second[h] + 1, 0, COLS), r2.at[s - 1, h, 0], dev2(h, 1))
            scatters[s, h, 1].wait_recv()
            add4(s, h, second[h] - 1, QUARTER, QUARTER, [r1.at[s - 1, h, 1]])
            ssend(s, h, 3, g4(s, h, second[h] - 1, 0, COLS), r2.at[s - 1, h, 1], dev2(h, -1))

    def scatter3(s):
        for h in (0, 1):
            scatters[s, h, 2].wait_recv()
            scatters[s, h, 3].wait_recv()
            add4(s, h, second[h], 0, COLS, [r2.at[s - 1, h, 0], r2.at[s - 1, h, 1]])
            far = first[h] + 2
            ssend(s, h, 4, g1(s, h, far, 0, QUARTER), r3.at[s - 1, h, 0], dev1(h, 1))
            ssend(s, h, 5, g1(s, h, far, QUARTER, QUARTER), r3.at[s - 1, h, 1], dev1(h, -1))

    def scatter4(s):
        for h in (0, 1):
            scatters[s, h, 4].wait_recv()
            sum1(s, h, first[h] + 1, 0, QUARTER, [r3.at[s - 1, h, 0]])
            ssend(s, h, 6, g1(s, h, first[h] + 1, 0, COLS), r4.at[s - 1, h, 0], dev1(h, 1))
            scatters[s, h, 5].wait_recv()
            sum1(s, h, first[h] - 1, QUARTER, QUARTER, [r3.at[s - 1, h, 1]])
            ssend(s, h, 7, g1(s, h, first[h] - 1, 0, COLS), r4.at[s - 1, h, 1], dev1(h, -1))

    def scatter5(s, mine_ref, other_ref):
        for h in (0, 1):
            scatters[s, h, 6].wait_recv()
            scatters[s, h, 7].wait_recv()
            sum1(s, h, first[h], 0, COLS, [r4.at[s - 1, h, 0], r4.at[s - 1, h, 1]])
        for c in range(0, HALF, TILE):
            cols = pl.ds(c, TILE)
            block = rows[s, mx, my, :, cols]
            mine_ref[:, cols] = lax.dot_general(
                place_mine, block, lead, preferred_element_type=F32
            ).astype(BF16)
            other_ref[:, cols] = lax.dot_general(
                place_other, block, lead, preferred_element_type=F32
            ).astype(BF16)

    token[B] = pack(B, upper, order_b, active_b, weight_b)
    fetched[F] = fetch(xf_ref, upper, 0)
    token[G] = pack(G, lower, order_b, active_b, weight_b)
    wu_in.append(up_part(1))
    wu_own = keep(up_ref.at[mine], wu.at[0], 4)
    wd_own = keep(down_ref.at[:, mine], wd.at[0], 5)
    token[F] = pack(F, upper, order_f, active_f, weight_f)
    wu_in.append(up_part(2))
    wu_in.append(up_part(3))
    fill(B)
    gather1(B)
    gather2(B)
    gather3(B)
    wd_in = zsend(down_ref.at[:, other], wd.at[1], 4)
    fill(G)
    gather1(G)
    gather2(G)
    gather4(B)
    gather3(G)
    fill(F)
    gather1(F)
    gather5(B)
    for copy in wu_in:
        copy.wait_recv()
    wu_own.wait()
    partial_up(B)
    gather4(G)
    gather2(F)
    gather3(F)
    fin = zsend(xf_ref, fin_ref, 10, (after, me))
    told = zsend(info, info_ref, 3, (after, me))
    gather5(G)
    wd_in.wait_recv()
    wd_own.wait()
    partial_back(G)
    gather4(F)
    gather5(F)
    partial_up(F)
    activate_back()
    down_grad()
    dg_out = zsend(dgs.at[1], dg_ref.at[:, mine], 5)
    dg_own = keep(dgs.at[0], dg_ref.at[:, mine], 6)
    gathered_out(G)
    rows_out(G, G, wu, last)
    scatter1(G)
    up_grad()
    ug_out = zsend(ugs.at[1], ug_ref.at[mine], 6)
    ug_own = keep(ugs.at[0], ug_ref.at[mine], 7)
    scatter2(G)
    activate_fwd()
    gathered_out(F)
    rows_out(F, F, wd, None)
    scatter1(F)
    scatter3(G)
    scatter2(F)
    scatter4(G)
    scatter3(F)
    token[B].wait_send()
    token[G].wait_send()
    token[F].wait_send()
    scatter5(G, local.at[0], local.at[1])
    row_own = keep(local.at[0], rout_ref.at[zh], 8)
    row_out = zsend(local.at[1], rout_ref.at[zh], 7)
    scatter4(F)
    scatter5(F, local.at[2], remote.at[0])
    near_out = zsend(local.at[2], fout_ref.at[zh], 8, (after, me))
    far_out = zsend(remote.at[0], fout_ref.at[zh], 9, (after, mate))

    for copy in (dg_own, ug_own, row_own):
        copy.wait()
    for copy in (dg_out, ug_out, row_out, near_out, far_out, fin, told):
        copy.wait()
    for copy in wu_in:
        copy.wait_send()
    wd_in.wait_send()
    gathered_out(B)
    for s in (G, F):
        for h in (0, 1):
            for k in range(8):
                scatters[s, h, k].wait_send()

    def done(n, carry):
        pre_copy(n // 4, n % 4).wait_send()
        return carry

    lax.fori_loop(0, 12, done, 0)


def relay(plan, xb, xg, xf, upper, lower):
    hbm = pl.BlockSpec(memory_space=pl.ANY)
    shapes = [
        jax.ShapeDtypeStruct(xf.shape, BF16),
        jax.ShapeDtypeStruct((2, SLOTS, HALF), BF16),
        jax.ShapeDtypeStruct((2, SLOTS, HALF), BF16),
        jax.ShapeDtypeStruct(upper.shape, BF16),
        jax.ShapeDtypeStruct(lower.shape, BF16),
        jax.ShapeDtypeStruct((8, TOKENS), F32),
    ]
    dma = pltpu.SemaphoreType.DMA
    return pl.pallas_call(
        kernel,
        out_shape=shapes,
        in_specs=[pl.BlockSpec(memory_space=pltpu.VMEM)] + [hbm] * 5,
        out_specs=[hbm] * 6,
        scratch_shapes=[
            pltpu.VMEM((8, TOKENS), F32),
            pltpu.VMEM((3, 4, 4, BLOCK, HALF), BF16),
            pltpu.VMEM((2, HALF, UNITS), BF16),
            pltpu.VMEM((2, UNITS, HALF), BF16),
            pltpu.VMEM((3, SLOTS, HALF), BF16),
            pltpu.VMEM((3, SLOTS, HALF), BF16),
            pltpu.VMEM((3, 4, 4 * BLOCK, 2 * UNITS), BF16),
            pltpu.VMEM((3, 4, 4 * BLOCK, 2 * UNITS), BF16),
            pltpu.VMEM((2, UNITS, HALF), BF16),
            pltpu.VMEM((2, HALF, UNITS), BF16),
            pltpu.VMEM((2, 2, 2, 4, BLOCK, QUARTER), BF16),
            pltpu.VMEM((2, 2, 2, 4, BLOCK, COLS), BF16),
            pltpu.VMEM((2, 2, 2, BLOCK, QUARTER), BF16),
            pltpu.VMEM((2, 2, 2, BLOCK, COLS), BF16),
            dma((3, 2, 8)),
            dma((3, 2, 8)),
            dma((2, 2, 8)),
            dma((2, 2, 8)),
            dma((3, 4)),
            dma((3, 4)),
            dma((15,)),
            dma((15,)),
            dma((9,)),
        ],
        compiler_params=pltpu.CompilerParams(
            collective_id=0, has_side_effects=True, vmem_limit_bytes=64 * 1024 * 1024
        ),
        cost_estimate=pl.CostEstimate(
            flops=28_000_000_000, bytes_accessed=40_000_000, transcendentals=2_000_000
        ),
        name="relay",
    )(plan, xb, xg, xf, upper, lower)


def column(line):
    down = lax.broadcasted_iota(jnp.int32, (TOKENS, TOKENS), 0)
    across = lax.broadcasted_iota(jnp.int32, (TOKENS, TOKENS), 1)
    return jnp.sum(jnp.where(down == across, line, 0.0), axis=1, keepdims=True)


def finish_kernel(
    plan_ref, info_ref, xg_ref, fin_ref, fout_ref, rout_ref, ug_ref, dg_ref, next_ref, grad_ref, up_ref, down_ref, sem
):
    copies = [
        pltpu.make_async_copy(ug_ref, up_ref, sem.at[0]),
        pltpu.make_async_copy(dg_ref, down_ref, sem.at[1]),
    ]
    for copy in copies:
        copy.start()
    expert = lax.axis_index("section").astype(F32)
    order, active, _ = route(plan_ref, 4, expert)
    lead = (((0,), (0,)), ((), ()))
    place = lax.broadcasted_iota(jnp.int32, (SLOTS, TOKENS), 0).astype(F32)
    mine = jnp.where((order == place) & (active > 0.0), 1.0, 0.0).astype(BF16)
    theirs = jnp.where(info_ref[0:1, :] == place, 1.0, 0.0).astype(BF16)
    weight = column(info_ref[1:2, :])
    for half in (0, 1):
        for c in range(0, HALF, TILE):
            here, there = pl.ds(c, TILE), pl.ds(half * HALF + c, TILE)
            spread = lax.dot_general(theirs, fout_ref[half, :, here], lead, preferred_element_type=F32)
            next_ref[:, there] = (fin_ref[:, there].astype(F32) + weight * spread).astype(BF16)
            spread = lax.dot_general(mine, rout_ref[half, :, here], lead, preferred_element_type=F32)
            grad_ref[:, there] = (xg_ref[:, there].astype(F32) + spread).astype(BF16)
    for copy in copies:
        copy.wait()


def finish(plan, info, xg, fin, fout, rout, up_grad, down_grad):
    hbm = pl.BlockSpec(memory_space=pl.ANY)
    vmem = pl.BlockSpec(memory_space=pltpu.VMEM)
    return pl.pallas_call(
        finish_kernel,
        out_shape=[jax.ShapeDtypeStruct(a.shape, BF16) for a in (fin, xg, up_grad, down_grad)],
        in_specs=[vmem] * 6 + [hbm] * 2,
        out_specs=[vmem] * 2 + [hbm] * 2,
        scratch_shapes=[pltpu.SemaphoreType.DMA((2,))],
        compiler_params=pltpu.CompilerParams(vmem_limit_bytes=64 * 1024 * 1024),
        cost_estimate=pl.CostEstimate(
            flops=150_000_000, bytes_accessed=20_000_000, transcendentals=0
        ),
        name="finish",
    )(plan, info, xg, fin, fout, rout, up_grad, down_grad)


def body(
    fwd_input,
    fwd_routes,
    fwd_weights,
    bwd_input,
    bwd_routes,
    bwd_weights,
    out_grad,
    up_weight,
    down_weight,
):
    lines = [fwd_routes[0].T, fwd_weights[0].T, bwd_routes[0].T, bwd_weights[0].T]
    plan = jnp.concatenate([line.astype(F32) for line in lines], axis=0)
    fin, fout, rout, up_grad, down_grad, info = relay(
        plan, bwd_input[0], out_grad[0], fwd_input[0], up_weight[0], down_weight[0]
    )
    outs = finish(plan, info, out_grad[0], fin, fout, rout, up_grad, down_grad)
    return tuple(out[None] for out in outs)


def solution(mesh):
    row_spec = P("section", "fsdp", None)
    in_specs = (row_spec,) * 7 + (P("section", None, "fsdp"), row_spec)
    out_specs = (row_spec, row_spec, P("section", None, "fsdp"), row_spec)
    return jax.shard_map(body, mesh=mesh, in_specs=in_specs, out_specs=out_specs, check_vma=False)
```

```python
import functools

import jax
import jax.numpy as jnp
from jax import lax
from jax.experimental import pallas as pl
from jax.experimental.pallas import tpu as pltpu
from jax.sharding import PartitionSpec as P

MESH = pl.DeviceIdType.MESH
F32 = jnp.float32
BF16 = jnp.bfloat16

CAP = 40
SLOTS = 48
D = 6144
HALF = D // 2
UNITS = 256
TOKENS = 128
BLOCK = 2 * CAP
COLS = HALF // 2
QUARTER = COLS // 2
TILE = 768

EXTRA = 1536
KEPT = HALF - EXTRA
B, G, F, X = 0, 1, 2, 3


def route(plan_ref, base, expert):
    hit = [plan_ref[pl.ds(base + k, 1), :] == expert for k in (0, 1)]
    share = [plan_ref[pl.ds(base + 2 + k, 1), :] for k in (0, 1)]
    active = jnp.where(hit[0] | hit[1], 1.0, 0.0)
    weight = jnp.where(hit[0], share[0], 0.0) + jnp.where(hit[1], share[1], 0.0)
    earlier = lax.broadcasted_iota(jnp.int32, (TOKENS, TOKENS), 0)
    later = lax.broadcasted_iota(jnp.int32, (TOKENS, TOKENS), 1)
    before = jnp.where(earlier < later, 1.0, 0.0).astype(BF16)
    spread = jnp.broadcast_to(active, (8, TOKENS)).astype(BF16)
    order = jnp.dot(spread, before, preferred_element_type=F32)[0:1]
    return order, active, weight


def kernel(
    plan_ref,
    xb_ref,
    xg_ref,
    xf_ref,
    up_ref,
    down_ref,
    fin_ref,
    fout_ref,
    rout_ref,
    ug_ref,
    dg_ref,
    info_ref,
    info,
    rows,
    extra,
    sent,
    got,
    wu,
    wd,
    local,
    remote,
    part,
    peer,
    dgs,
    ugs,
    r1,
    r2,
    r3,
    r4,
    ag_send,
    ag_recv,
    rs_send,
    rs_recv,
    pre_send,
    pre_recv,
    z_send,
    z_recv,
    loc_sem,
):
    sec = lax.axis_index("section")
    me = lax.axis_index("fsdp")
    mx = me // 8
    my = (me // 2) % 4
    zh = me % 2
    mate = me + 1 - 2 * zh
    after = (sec + 1) % 4
    before = (sec + 3) % 4

    def at(x, y):
        return (sec, (((x + 4) % 4) * 4 + (y + 4) % 4) * 2 + zh)

    pair = (sec, mate)

    barrier = pltpu.get_barrier_semaphore()
    near = [
        at(mx + 1, my),
        at(mx - 1, my),
        at(mx, my + 1),
        at(mx, my - 1),
        pair,
        (after, me),
        (after, mate),
        (before, me),
        (before, mate),
    ]
    for device in near:
        pl.semaphore_signal(barrier, inc=1, device_id=device, device_id_type=MESH)
    pl.semaphore_wait(barrier, len(near))

    mine = pl.ds(pl.multiple_of(zh * HALF, HALF), HALF)
    other = pl.ds(pl.multiple_of((1 - zh) * HALF, HALF), HALF)
    started = []

    def send(src, dst, send_sem, recv_sem, device):
        copy = pltpu.make_async_remote_copy(
            src_ref=src,
            dst_ref=dst,
            send_sem=send_sem,
            recv_sem=recv_sem,
            device_id=device,
            device_id_type=MESH,
        )
        copy.start()
        return copy

    def keep(src, dst, index):
        copy = pltpu.make_async_copy(src, dst, loc_sem.at[index])
        copy.start()
        return copy

    def zsend(src, dst, index, device=pair):
        return send(src, dst, z_send.at[index], z_recv.at[index], device)

    def up_part(n):
        width = HALF // 4
        start = pl.multiple_of((1 - zh) * HALF + n * width, width)
        return zsend(up_ref.at[pl.ds(start, width)], wu.at[1, pl.ds(n * width, width)], 11 + n)

    wu_in = [up_part(0)]
    upper, lower = pl.ds(0, TOKENS), pl.ds(TOKENS, TOKENS)

    def fetch(source, where, index):
        return [
            keep(source.at[:, pl.ds(half * HALF, HALF)], dgs.at[half, where], index + half)
            for half in (0, 1)
        ]

    fetched = {F: fetch(xf_ref, upper, 0), B: fetch(xb_ref, lower, 2)}

    token = {}

    def selector(order, active, count, offset):
        place = lax.broadcasted_iota(jnp.int32, (count, TOKENS), 0).astype(F32)
        return jnp.where((order + offset == place) & (active > 0.0), 1.0, 0.0)

    expert = sec.astype(F32)
    order_b, active_b, weight_b = route(plan_ref, 4, expert)
    order_f, active_f, weight_f = route(plan_ref, 0, expert)
    shift = (CAP * zh).astype(F32)
    line = lax.broadcasted_iota(jnp.int32, (8, TOKENS), 0)
    slots_f = jnp.where(active_f > 0.0, order_f, -1.0)
    info[...] = jnp.where(line == 0, slots_f, jnp.where(line == 1, weight_f, 0.0))

    slot = lax.broadcasted_iota(jnp.int32, (BLOCK, SLOTS), 1)
    row = lax.broadcasted_iota(jnp.int32, (BLOCK, SLOTS), 0)

    def place(which):
        hit = (row == slot + CAP * which) & (slot < CAP)
        return jnp.where(hit, 1.0, 0.0).astype(BF16)

    place_mine, place_other = place(zh), place(1 - zh)

    def pack(s, where, order, active, weight):
        for copy in fetched[s]:
            copy.wait()
        small = selector(order, active, SLOTS, 0.0)
        wide = selector(order, active, BLOCK, shift)
        small_w = jnp.sum(small * weight, axis=1, keepdims=True)
        wide_w = jnp.sum(wide * weight, axis=1, keepdims=True)
        for c in range(0, HALF, TILE):
            cols = pl.ds(c, TILE)
            value = jnp.dot(small.astype(BF16), dgs[1 - zh, where, cols], preferred_element_type=F32)
            if s == G:
                value = value * small_w
            local[s, :, cols] = value.astype(BF16)
        copy = zsend(local.at[s], remote.at[s], s)
        if s == G:
            for c in range(0, EXTRA, TILE):
                value = jnp.dot(
                    small.astype(BF16), dgs[zh, where, pl.ds(KEPT + c, TILE)], preferred_element_type=F32
                )
                sent[:, pl.ds(c, TILE)] = (value * small_w).astype(BF16)
            token[X] = zsend(sent, got, 15)
        for c in range(0, HALF, TILE):
            cols = pl.ds(c, TILE)
            value = jnp.dot(wide.astype(BF16), dgs[zh, where, cols], preferred_element_type=F32)
            if s == G:
                value = value * wide_w
            rows[s, mx, my, :, cols] = value.astype(BF16)
        return copy

    def fill_extra():
        token[X].wait_recv()
        for c in range(0, EXTRA, TILE):
            cols = pl.ds(c, TILE)
            total = jnp.dot(place_other, got[:, cols], preferred_element_type=F32)
            total += jnp.dot(
                place_mine, local[G, :, pl.ds(KEPT + c, TILE)], preferred_element_type=F32
            )
            extra[mx, my, :, cols] = total.astype(BF16)

    def fill(s):
        token[s].wait_recv()
        for c in range(0, HALF, TILE):
            cols = pl.ds(c, TILE)
            total = jnp.dot(place_other, remote[s, :, cols], preferred_element_type=F32)
            total += rows[s, mx, my, :, cols].astype(F32)
            rows[s, mx, my, :, cols] = total.astype(BF16)

    def up4(i):
        return (i + 4) % 4

    def one(h, i):
        return (up4(i), my) if h == 0 else (mx, up4(i))

    def span(s):
        return EXTRA // 2 if s == X else COLS

    def g1(s, h, i, start, width):
        x, y = one(h, i)
        if s == X:
            return extra.at[x, y, :, pl.ds(h * span(s) + start, width)]
        return rows.at[s, x, y, :, pl.ds(h * COLS + start, width)]

    def g4(s, h, j, start, width):
        cols = pl.ds(h * span(s) + start, width)
        if s == X:
            return extra.at[:, up4(j), :, cols] if h == 0 else extra.at[up4(j), :, :, cols]
        if h == 0:
            return rows.at[s, :, up4(j), :, cols]
        return rows.at[s, up4(j), :, :, cols]

    first, second = (mx, my), (my, mx)

    def dev1(h, step):
        return at(mx + step, my) if h == 0 else at(mx, my + step)

    def dev2(h, step):
        return at(mx, my + step) if h == 0 else at(mx + step, my)

    gathers = {}

    def gsend(s, h, k, ref, device):
        gathers[s, h, k] = send(ref, ref, ag_send.at[s, h, k], ag_recv.at[s, h, k], device)

    def gather1(s):
        for h in (0, 1):
            ref = g1(s, h, first[h], 0, span(s))
            gsend(s, h, 0, ref, dev1(h, 1))
            gsend(s, h, 1, ref, dev1(h, -1))

    def gather2(s):
        for h in (0, 1):
            gathers[s, h, 0].wait_recv()
            gsend(s, h, 2, g1(s, h, first[h] - 1, 0, span(s) // 2), dev1(h, 1))
            gathers[s, h, 1].wait_recv()
            gsend(s, h, 3, g1(s, h, first[h] + 1, span(s) // 2, span(s) // 2), dev1(h, -1))

    def gather3(s):
        for h in (0, 1):
            gathers[s, h, 2].wait_recv()
            gathers[s, h, 3].wait_recv()
            ref = g4(s, h, second[h], 0, span(s))
            gsend(s, h, 4, ref, dev2(h, 1))
            gsend(s, h, 5, ref, dev2(h, -1))

    def gather4(s):
        for h in (0, 1):
            gathers[s, h, 4].wait_recv()
            gsend(s, h, 6, g4(s, h, second[h] - 1, 0, span(s) // 2), dev2(h, 1))
            gathers[s, h, 5].wait_recv()
            gsend(s, h, 7, g4(s, h, second[h] + 1, span(s) // 2, span(s) // 2), dev2(h, -1))

    def gather5(s):
        for h in (0, 1):
            gathers[s, h, 6].wait_recv()
            gathers[s, h, 7].wait_recv()

    def gathered_out(s):
        for h in (0, 1):
            for k in range(8):
                gathers[s, h, k].wait_send()

    def pre_copy(s, i):
        return pltpu.make_async_remote_copy(
            src_ref=part.at[s, i],
            dst_ref=peer.at[s, i],
            send_sem=pre_send.at[s, i],
            recv_sem=pre_recv.at[s, i],
            device_id=pair,
            device_id_type=MESH,
        )

    last = (((1,), (1,)), ((), ()))
    lead = (((0,), (0,)), ((), ()))

    def partial_up(s):
        def step(i, carry):
            block = rows[s, i].reshape(4 * BLOCK, HALF)
            for u in (0, 1):
                value = jnp.dot(block, wu[u], preferred_element_type=F32)
                part[s, i, :, pl.ds(u * UNITS, UNITS)] = value.astype(BF16)
            pre_copy(s, i).start()
            return carry

        lax.fori_loop(0, 4, step, 0)

    def partial_back(s):
        def step(i, carry):
            block = rows[s, i].reshape(4 * BLOCK, HALF)
            for u in (0, 1):
                value = lax.dot_general(block, wd[u], last, preferred_element_type=F32)
                part[s, i, :, pl.ds(u * UNITS, UNITS)] = value.astype(BF16)
            pre_copy(s, i).start()
            return carry

        lax.fori_loop(0, 4, step, 0)

    def whole(s, i, u):
        here = part[s, i, :, pl.ds(u * UNITS, UNITS)].astype(F32)
        return here + peer[s, i, :, pl.ds((1 - u) * UNITS, UNITS)].astype(F32)

    def sigmoid(value):
        return 1.0 / (1.0 + jnp.exp(-value))

    def activate_back():
        def step(i, carry):
            pre_copy(B, i).wait_recv()
            pre_copy(B, i).wait_send()
            hidden, slope = [], []
            for u in (0, 1):
                pre = whole(B, i, u)
                gate = sigmoid(pre)
                hidden.append((pre * gate).astype(BF16))
                slope.append((gate * (1.0 + pre * (1.0 - gate))).astype(BF16))
            for u in (0, 1):
                peer[B, i, :, pl.ds(u * UNITS, UNITS)] = hidden[u]
                part[B, i, :, pl.ds(u * UNITS, UNITS)] = slope[u]
            return carry

        lax.fori_loop(0, 4, step, 0)

    def back_grad():
        def step(i, carry):
            pre_copy(G, i).wait_recv()
            value = []
            for u in (0, 1):
                slope = part[B, i, :, pl.ds(u * UNITS, UNITS)].astype(F32)
                value.append((whole(G, i, u) * slope).astype(BF16))
            for u in (0, 1):
                peer[G, i, :, pl.ds(u * UNITS, UNITS)] = value[u]
            return carry

        lax.fori_loop(0, 4, step, 0)

    def activate_fwd():
        def step(i, carry):
            pre_copy(F, i).wait_recv()
            hidden = []
            for u in (0, 1):
                pre = whole(F, i, u)
                hidden.append((pre * sigmoid(pre)).astype(BF16))
            for u in (0, 1):
                peer[F, i, :, pl.ds(u * UNITS, UNITS)] = hidden[u]
            return carry

        lax.fori_loop(0, 4, step, 0)

    def down_grad():
        for u, width in ((1, KEPT), (0, HALF)):
            def step(c, carry):
                cols = pl.ds(pl.multiple_of(c * TILE, TILE), TILE)
                left = peer[B, :, :, pl.ds(u * UNITS, UNITS)].reshape(16 * BLOCK, UNITS)
                right = rows[G, :, :, :, cols].reshape(16 * BLOCK, TILE)
                value = lax.dot_general(left, right, lead, preferred_element_type=F32)
                dgs[u, :, cols] = value.astype(BF16)
                return carry

            lax.fori_loop(0, width // TILE, step, 0)

    def down_grad_extra():
        def step(c, carry):
            start = pl.multiple_of(c * TILE, TILE)
            left = peer[B, :, :, pl.ds(0, UNITS)].reshape(16 * BLOCK, UNITS)
            right = extra[:, :, :, pl.ds(start, TILE)].reshape(16 * BLOCK, TILE)
            value = lax.dot_general(left, right, lead, preferred_element_type=F32)
            dgs[1, :, pl.ds(KEPT + start, TILE)] = value.astype(BF16)
            return carry

        lax.fori_loop(0, EXTRA // TILE, step, 0)

    def up_grad():
        def step(c, carry):
            cols = pl.ds(pl.multiple_of(c * TILE, TILE), TILE)
            left = rows[B, :, :, :, cols].reshape(16 * BLOCK, TILE)
            for u in (0, 1):
                right = peer[G, :, :, pl.ds(u * UNITS, UNITS)].reshape(16 * BLOCK, UNITS)
                value = lax.dot_general(left, right, lead, preferred_element_type=F32)
                ugs[u, cols, :] = value.astype(BF16)
            return carry

        lax.fori_loop(0, HALF // TILE, step, 0)

    def rows_out(s, source, weights, dims):
        def step(n, carry):
            i = n // (HALF // TILE)
            c = n % (HALF // TILE)
            cols = pl.ds(pl.multiple_of(c * TILE, TILE), TILE)
            total = None
            for u in (0, 1):
                left = peer[source, i, :, pl.ds(u * UNITS, UNITS)]
                right = weights[u, cols, :] if dims == last else weights[u, :, cols]
                if dims == last:
                    value = lax.dot_general(left, right, last, preferred_element_type=F32)
                else:
                    value = jnp.dot(left, right, preferred_element_type=F32)
                total = value if total is None else total + value
            rows[s, i, :, :, cols] = total.astype(BF16).reshape(4, BLOCK, TILE)
            return carry

        lax.fori_loop(0, 4 * (HALF // TILE), step, 0)

    scatters = {}

    def ssend(s, h, k, src, dst, device):
        scatters[s, h, k] = send(src, dst, rs_send.at[s - 1, h, k], rs_recv.at[s - 1, h, k], device)

    def add4(s, h, j, start, width, sources):
        cols = pl.ds(h * COLS + start, width)

        def step(i, carry):
            x, y = (i, up4(j)) if h == 0 else (up4(j), i)
            total = rows[s, x, y, :, cols].astype(F32)
            for source in sources:
                total += source[i].astype(F32)
            rows[s, x, y, :, cols] = total.astype(BF16)
            return carry

        lax.fori_loop(0, 4, step, 0)

    def sum1(s, h, i, start, width, sources):
        x, y = one(h, i)
        total = rows[s, x, y, :, pl.ds(h * COLS + start, width)].astype(F32)
        for source in sources:
            total += source[...].astype(F32)
        rows[s, x, y, :, pl.ds(h * COLS + start, width)] = total.astype(BF16)

    def scatter1(s):
        for h in (0, 1):
            far = second[h] + 2
            ssend(s, h, 0, g4(s, h, far, 0, QUARTER), r1.at[s - 1, h, 0], dev2(h, 1))
            ssend(s, h, 1, g4(s, h, far, QUARTER, QUARTER), r1.at[s - 1, h, 1], dev2(h, -1))

    def scatter2(s):
        for h in (0, 1):
            scatters[s, h, 0].wait_recv()
            add4(s, h, second[h] + 1, 0, QUARTER, [r1.at[s - 1, h, 0]])
            ssend(s, h, 2, g4(s, h, second[h] + 1, 0, COLS), r2.at[s - 1, h, 0], dev2(h, 1))
            scatters[s, h, 1].wait_recv()
            add4(s, h, second[h] - 1, QUARTER, QUARTER, [r1.at[s - 1, h, 1]])
            ssend(s, h, 3, g4(s, h, second[h] - 1, 0, COLS), r2.at[s - 1, h, 1], dev2(h, -1))

    def scatter3(s):
        for h in (0, 1):
            scatters[s, h, 2].wait_recv()
            scatters[s, h, 3].wait_recv()
            add4(s, h, second[h], 0, COLS, [r2.at[s - 1, h, 0], r2.at[s - 1, h, 1]])
            far = first[h] + 2
            ssend(s, h, 4, g1(s, h, far, 0, QUARTER), r3.at[s - 1, h, 0], dev1(h, 1))
            ssend(s, h, 5, g1(s, h, far, QUARTER, QUARTER), r3.at[s - 1, h, 1], dev1(h, -1))

    def scatter4(s):
        for h in (0, 1):
            scatters[s, h, 4].wait_recv()
            sum1(s, h, first[h] + 1, 0, QUARTER, [r3.at[s - 1, h, 0]])
            ssend(s, h, 6, g1(s, h, first[h] + 1, 0, COLS), r4.at[s - 1, h, 0], dev1(h, 1))
            scatters[s, h, 5].wait_recv()
            sum1(s, h, first[h] - 1, QUARTER, QUARTER, [r3.at[s - 1, h, 1]])
            ssend(s, h, 7, g1(s, h, first[h] - 1, 0, COLS), r4.at[s - 1, h, 1], dev1(h, -1))

    def scatter5(s, mine_ref, other_ref):
        for h in (0, 1):
            scatters[s, h, 6].wait_recv()
            scatters[s, h, 7].wait_recv()
            sum1(s, h, first[h], 0, COLS, [r4.at[s - 1, h, 0], r4.at[s - 1, h, 1]])
        for c in range(0, HALF, TILE):
            cols = pl.ds(c, TILE)
            block = rows[s, mx, my, :, cols]
            mine_ref[:, cols] = lax.dot_general(
                place_mine, block, lead, preferred_element_type=F32
            ).astype(BF16)
            other_ref[:, cols] = lax.dot_general(
                place_other, block, lead, preferred_element_type=F32
            ).astype(BF16)

    token[F] = pack(F, upper, order_f, active_f, weight_f)
    fetched[G] = fetch(xg_ref, upper, 0)
    token[B] = pack(B, lower, order_b, active_b, weight_b)
    wu_in.append(up_part(1))
    wu_own = keep(up_ref.at[mine], wu.at[0], 4)
    wd_own = keep(down_ref.at[:, mine], wd.at[0], 5)
    token[G] = pack(G, upper, order_b, active_b, weight_b)
    wu_in.append(up_part(2))
    wu_in.append(up_part(3))
    fill(F)
    gather1(F)
    gather2(F)
    gather3(F)
    wd_in = zsend(down_ref.at[:, other], wd.at[1], 4)
    fill(B)
    gather1(B)
    gather2(B)
    gather4(F)
    gather3(B)
    fill(G)
    gather1(G)
    gather5(F)
    fill_extra()
    for copy in wu_in:
        copy.wait_recv()
    wu_own.wait()
    partial_up(F)
    gather4(B)
    gather2(G)
    gather3(G)
    gather5(B)
    partial_up(B)
    gather4(G)
    gather1(X)
    gather2(X)
    gather3(X)
    activate_fwd()
    gathered_out(F)
    wd_in.wait_recv()
    wd_own.wait()
    rows_out(F, F, wd, None)
    scatter1(F)
    gather5(G)
    partial_back(G)
    scatter2(F)
    activate_back()
    gather4(X)
    down_grad()
    kept = pl.ds(pl.multiple_of(zh * HALF, HALF), KEPT)
    dg_out = zsend(dgs.at[1, :, pl.ds(0, KEPT)], dg_ref.at[:, kept], 5)
    dg_own = keep(dgs.at[0], dg_ref.at[:, mine], 6)
    gathered_out(G)
    scatter3(F)
    fin = zsend(xf_ref, fin_ref, 10, (after, me))
    told = zsend(info, info_ref, 3, (after, me))
    back_grad()
    rows_out(G, G, wu, last)
    scatter1(G)
    up_grad()
    ug_out = zsend(ugs.at[1], ug_ref.at[mine], 6)
    ug_own = keep(ugs.at[0], ug_ref.at[mine], 7)
    gather5(X)
    down_grad_extra()
    far = pl.ds(pl.multiple_of((1 - zh) * HALF + KEPT, EXTRA), EXTRA)
    dg_far = keep(dgs.at[1, :, pl.ds(KEPT, EXTRA)], dg_ref.at[:, far], 9)
    scatter4(F)
    scatter2(G)
    token[B].wait_send()
    token[G].wait_send()
    token[F].wait_send()
    token[X].wait_send()
    scatter5(F, local.at[2], remote.at[0])
    near_out = zsend(local.at[2], fout_ref.at[zh], 8, (after, me))
    far_out = zsend(remote.at[0], fout_ref.at[zh], 9, (after, mate))
    scatter3(G)
    scatter4(G)
    scatter5(G, local.at[0], local.at[1])
    row_own = keep(local.at[0], rout_ref.at[zh], 8)
    row_out = zsend(local.at[1], rout_ref.at[zh], 7)

    for copy in (dg_own, dg_far, ug_own, row_own):
        copy.wait()
    for copy in (dg_out, ug_out, row_out, near_out, far_out, fin, told):
        copy.wait()
    for copy in wu_in:
        copy.wait_send()
    wd_in.wait_send()
    gathered_out(B)
    gathered_out(X)
    for s in (G, F):
        for h in (0, 1):
            for k in range(8):
                scatters[s, h, k].wait_send()

    def done(n, carry):
        pre_copy(n // 4, n % 4).wait_send()
        return carry

    lax.fori_loop(4, 12, done, 0)


def relay(plan, xb, xg, xf, upper, lower):
    hbm = pl.BlockSpec(memory_space=pl.ANY)
    shapes = [
        jax.ShapeDtypeStruct(xf.shape, BF16),
        jax.ShapeDtypeStruct((2, SLOTS, HALF), BF16),
        jax.ShapeDtypeStruct((2, SLOTS, HALF), BF16),
        jax.ShapeDtypeStruct(upper.shape, BF16),
        jax.ShapeDtypeStruct(lower.shape, BF16),
        jax.ShapeDtypeStruct((8, TOKENS), F32),
    ]
    dma = pltpu.SemaphoreType.DMA
    return pl.pallas_call(
        kernel,
        out_shape=shapes,
        in_specs=[pl.BlockSpec(memory_space=pltpu.VMEM)] + [hbm] * 5,
        out_specs=[hbm] * 6,
        scratch_shapes=[
            pltpu.VMEM((8, TOKENS), F32),
            pltpu.VMEM((3, 4, 4, BLOCK, HALF), BF16),
            pltpu.VMEM((4, 4, BLOCK, EXTRA), BF16),
            pltpu.VMEM((SLOTS, EXTRA), BF16),
            pltpu.VMEM((SLOTS, EXTRA), BF16),
            pltpu.VMEM((2, HALF, UNITS), BF16),
            pltpu.VMEM((2, UNITS, HALF), BF16),
            pltpu.VMEM((3, SLOTS, HALF), BF16),
            pltpu.VMEM((3, SLOTS, HALF), BF16),
            pltpu.VMEM((3, 4, 4 * BLOCK, 2 * UNITS), BF16),
            pltpu.VMEM((3, 4, 4 * BLOCK, 2 * UNITS), BF16),
            pltpu.VMEM((2, UNITS, HALF), BF16),
            pltpu.VMEM((2, HALF, UNITS), BF16),
            pltpu.VMEM((2, 2, 2, 4, BLOCK, QUARTER), BF16),
            pltpu.VMEM((2, 2, 2, 4, BLOCK, COLS), BF16),
            pltpu.VMEM((2, 2, 2, BLOCK, QUARTER), BF16),
            pltpu.VMEM((2, 2, 2, BLOCK, COLS), BF16),
            dma((4, 2, 8)),
            dma((4, 2, 8)),
            dma((2, 2, 8)),
            dma((2, 2, 8)),
            dma((3, 4)),
            dma((3, 4)),
            dma((16,)),
            dma((16,)),
            dma((10,)),
        ],
        compiler_params=pltpu.CompilerParams(
            collective_id=0, has_side_effects=True, vmem_limit_bytes=64 * 1024 * 1024
        ),
        cost_estimate=pl.CostEstimate(
            flops=28_000_000_000, bytes_accessed=40_000_000, transcendentals=2_000_000
        ),
        name="relay",
    )(plan, xb, xg, xf, upper, lower)


def column(line):
    down = lax.broadcasted_iota(jnp.int32, (TOKENS, TOKENS), 0)
    across = lax.broadcasted_iota(jnp.int32, (TOKENS, TOKENS), 1)
    return jnp.sum(jnp.where(down == across, line, 0.0), axis=1, keepdims=True)


def finish_kernel(
    plan_ref, info_ref, xg_ref, fin_ref, fout_ref, rout_ref, ug_ref, dg_ref, next_ref, grad_ref, up_ref, down_ref, up_held, down_held, sem
):
    loads, stores = [], []
    for n in range(4):
        for k, (src, held, dst) in enumerate(((ug_ref, up_held, up_ref), (dg_ref, down_held, down_ref))):
            part = pl.ds(n * (src.shape[0] // 4), src.shape[0] // 4)
            loads.append(pltpu.make_async_copy(src.at[part], held.at[part], sem.at[0, k, n]))
            stores.append(pltpu.make_async_copy(held.at[part], dst.at[part], sem.at[1, k, n]))
    for load in loads:
        load.start()
    expert = lax.axis_index("section").astype(F32)
    order, active, _ = route(plan_ref, 4, expert)
    lead = (((0,), (0,)), ((), ()))
    place = lax.broadcasted_iota(jnp.int32, (SLOTS, TOKENS), 0).astype(F32)
    mine = jnp.where((order == place) & (active > 0.0), 1.0, 0.0).astype(BF16)
    theirs = jnp.where(info_ref[0:1, :] == place, 1.0, 0.0).astype(BF16)
    weight = column(info_ref[1:2, :])
    moves = iter(zip(loads, stores))
    for half in (0, 1):
        for c in range(0, HALF, TILE):
            here, there = pl.ds(c, TILE), pl.ds(half * HALF + c, TILE)
            spread = lax.dot_general(theirs, fout_ref[half, :, here], lead, preferred_element_type=F32)
            next_ref[:, there] = (fin_ref[:, there].astype(F32) + weight * spread).astype(BF16)
            spread = lax.dot_general(mine, rout_ref[half, :, here], lead, preferred_element_type=F32)
            grad_ref[:, there] = (xg_ref[:, there].astype(F32) + spread).astype(BF16)
            load, store = next(moves)
            load.wait()
            store.start()
    for store in stores:
        store.wait()


def finish(plan, info, xg, fin, fout, rout, up_grad, down_grad):
    hbm = pl.BlockSpec(memory_space=pl.ANY)
    vmem = pl.BlockSpec(memory_space=pltpu.VMEM)
    return pl.pallas_call(
        finish_kernel,
        out_shape=[jax.ShapeDtypeStruct(a.shape, BF16) for a in (fin, xg, up_grad, down_grad)],
        in_specs=[vmem] * 6 + [hbm] * 2,
        out_specs=[vmem] * 2 + [hbm] * 2,
        scratch_shapes=[
            pltpu.VMEM(up_grad.shape, BF16),
            pltpu.VMEM(down_grad.shape, BF16),
            pltpu.SemaphoreType.DMA((2, 2, 4)),
        ],
        compiler_params=pltpu.CompilerParams(vmem_limit_bytes=64 * 1024 * 1024),
        cost_estimate=pl.CostEstimate(
            flops=150_000_000, bytes_accessed=20_000_000, transcendentals=0
        ),
        name="finish",
    )(plan, info, xg, fin, fout, rout, up_grad, down_grad)


def body(
    fwd_input,
    fwd_routes,
    fwd_weights,
    bwd_input,
    bwd_routes,
    bwd_weights,
    out_grad,
    up_weight,
    down_weight,
):
    lines = [fwd_routes[0].T, fwd_weights[0].T, bwd_routes[0].T, bwd_weights[0].T]
    plan = jnp.concatenate([line.astype(F32) for line in lines], axis=0)
    fin, fout, rout, up_grad, down_grad, info = relay(
        plan, bwd_input[0], out_grad[0], fwd_input[0], up_weight[0], down_weight[0]
    )
    outs = finish(plan, info, out_grad[0], fin, fout, rout, up_grad, down_grad)
    return tuple(out[None] for out in outs)


def solution(mesh):
    row_spec = P("section", "fsdp", None)
    in_specs = (row_spec,) * 7 + (P("section", None, "fsdp"), row_spec)
    out_specs = (row_spec, row_spec, P("section", None, "fsdp"), row_spec)
    return jax.shard_map(body, mesh=mesh, in_specs=in_specs, out_specs=out_specs, check_vma=False)
```

```python
import functools

import jax
import jax.numpy as jnp
from jax import lax
from jax.experimental import pallas as pl
from jax.experimental.pallas import tpu as pltpu
from jax.sharding import PartitionSpec as P

MESH = pl.DeviceIdType.MESH
F32 = jnp.float32
BF16 = jnp.bfloat16

CAP = 40
SLOTS = 48
D = 6144
HALF = D // 2
UNITS = 256
TOKENS = 128
BLOCK = 2 * CAP
COLS = HALF // 2
QUARTER = COLS // 2
TILE = 768

EXTRA = 1536
KEPT = HALF - EXTRA
B, G, F, X = 0, 1, 2, 3


def route(ids_ref, shares_ref, expert):
    hit = [ids_ref[pl.ds(k, 1), :] == expert for k in (0, 1)]
    share = [shares_ref[pl.ds(k, 1), :] for k in (0, 1)]
    active = jnp.where(hit[0] | hit[1], 1.0, 0.0)
    weight = jnp.where(hit[0], share[0], 0.0) + jnp.where(hit[1], share[1], 0.0)
    earlier = lax.broadcasted_iota(jnp.int32, (TOKENS, TOKENS), 0)
    later = lax.broadcasted_iota(jnp.int32, (TOKENS, TOKENS), 1)
    before = jnp.where(earlier < later, 1.0, 0.0).astype(BF16)
    spread = jnp.broadcast_to(active, (8, TOKENS)).astype(BF16)
    order = jnp.dot(spread, before, preferred_element_type=F32)[0:1]
    return order, active, weight


def kernel(
    ids_f_ref,
    shares_f_ref,
    ids_b_ref,
    shares_b_ref,
    xb_ref,
    xg_ref,
    xf_ref,
    up_ref,
    down_ref,
    fin_ref,
    fout_ref,
    rout_ref,
    ug_ref,
    dg_ref,
    info_ref,
    info,
    rows,
    extra,
    sent,
    got,
    wu,
    wd,
    local,
    remote,
    part,
    peer,
    dgs,
    ugs,
    r1,
    r2,
    r3,
    r4,
    ag_send,
    ag_recv,
    rs_send,
    rs_recv,
    pre_send,
    pre_recv,
    z_send,
    z_recv,
    loc_sem,
):
    sec = lax.axis_index("section")
    me = lax.axis_index("fsdp")
    mx = me // 8
    my = (me // 2) % 4
    zh = me % 2
    mate = me + 1 - 2 * zh
    after = (sec + 1) % 4
    before = (sec + 3) % 4

    def at(x, y):
        return (sec, (((x + 4) % 4) * 4 + (y + 4) % 4) * 2 + zh)

    pair = (sec, mate)

    barrier = pltpu.get_barrier_semaphore()
    near = [
        at(mx + 1, my),
        at(mx - 1, my),
        at(mx, my + 1),
        at(mx, my - 1),
        pair,
        (after, me),
        (after, mate),
        (before, me),
        (before, mate),
    ]
    for device in near:
        pl.semaphore_signal(barrier, inc=1, device_id=device, device_id_type=MESH)
    pl.semaphore_wait(barrier, len(near))

    mine = pl.ds(pl.multiple_of(zh * HALF, HALF), HALF)
    other = pl.ds(pl.multiple_of((1 - zh) * HALF, HALF), HALF)
    started = []

    def send(src, dst, send_sem, recv_sem, device):
        copy = pltpu.make_async_remote_copy(
            src_ref=src,
            dst_ref=dst,
            send_sem=send_sem,
            recv_sem=recv_sem,
            device_id=device,
            device_id_type=MESH,
        )
        copy.start()
        return copy

    def keep(src, dst, index):
        copy = pltpu.make_async_copy(src, dst, loc_sem.at[index])
        copy.start()
        return copy

    def zsend(src, dst, index, device=pair):
        return send(src, dst, z_send.at[index], z_recv.at[index], device)

    def up_part(n):
        width = HALF // 4
        start = pl.multiple_of((1 - zh) * HALF + n * width, width)
        return zsend(up_ref.at[pl.ds(start, width)], wu.at[1, pl.ds(n * width, width)], 11 + n)

    wu_in = [up_part(0)]
    upper, lower = pl.ds(0, TOKENS), pl.ds(TOKENS, TOKENS)

    def fetch(source, where, index):
        return [
            keep(source.at[:, pl.ds(half * HALF, HALF)], dgs.at[half, where], index + half)
            for half in (0, 1)
        ]

    fetched = {F: fetch(xf_ref, upper, 0), B: fetch(xb_ref, lower, 2)}

    token = {}

    def selector(order, active, count, offset):
        place = lax.broadcasted_iota(jnp.int32, (count, TOKENS), 0).astype(F32)
        return jnp.where((order + offset == place) & (active > 0.0), 1.0, 0.0)

    order_b, active_b, weight_b = route(ids_b_ref, shares_b_ref, sec)
    order_f, active_f, weight_f = route(ids_f_ref, shares_f_ref, sec)
    shift = (CAP * zh).astype(F32)
    line = lax.broadcasted_iota(jnp.int32, (8, TOKENS), 0)
    slots_f = jnp.where(active_f > 0.0, order_f, -1.0)
    info[...] = jnp.where(line == 0, slots_f, jnp.where(line == 1, weight_f, 0.0))

    slot = lax.broadcasted_iota(jnp.int32, (BLOCK, SLOTS), 1)
    row = lax.broadcasted_iota(jnp.int32, (BLOCK, SLOTS), 0)

    def place(which):
        hit = (row == slot + CAP * which) & (slot < CAP)
        return jnp.where(hit, 1.0, 0.0).astype(BF16)

    place_mine, place_other = place(zh), place(1 - zh)

    def pack(s, where, order, active, weight):
        for copy in fetched[s]:
            copy.wait()
        small = selector(order, active, SLOTS, 0.0)
        wide = selector(order, active, BLOCK, shift)
        small_w = jnp.sum(small * weight, axis=1, keepdims=True)
        wide_w = jnp.sum(wide * weight, axis=1, keepdims=True)
        for c in range(0, HALF, TILE):
            cols = pl.ds(c, TILE)
            value = jnp.dot(small.astype(BF16), dgs[1 - zh, where, cols], preferred_element_type=F32)
            if s == G:
                value = value * small_w
            local[s, :, cols] = value.astype(BF16)
        copy = zsend(local.at[s], remote.at[s], s)
        if s == G:
            for c in range(0, EXTRA, TILE):
                value = jnp.dot(
                    small.astype(BF16), dgs[zh, where, pl.ds(KEPT + c, TILE)], preferred_element_type=F32
                )
                sent[:, pl.ds(c, TILE)] = (value * small_w).astype(BF16)
            token[X] = zsend(sent, got, 15)
        for c in range(0, HALF, TILE):
            cols = pl.ds(c, TILE)
            value = jnp.dot(wide.astype(BF16), dgs[zh, where, cols], preferred_element_type=F32)
            if s == G:
                value = value * wide_w
            rows[s, mx, my, :, cols] = value.astype(BF16)
        return copy

    def fill_extra():
        token[X].wait_recv()
        for c in range(0, EXTRA, TILE):
            cols = pl.ds(c, TILE)
            total = jnp.dot(place_other, got[:, cols], preferred_element_type=F32)
            total += jnp.dot(
                place_mine, local[G, :, pl.ds(KEPT + c, TILE)], preferred_element_type=F32
            )
            extra[mx, my, :, cols] = total.astype(BF16)

    def fill(s):
        token[s].wait_recv()
        for c in range(0, HALF, TILE):
            cols = pl.ds(c, TILE)
            total = jnp.dot(place_other, remote[s, :, cols], preferred_element_type=F32)
            total += rows[s, mx, my, :, cols].astype(F32)
            rows[s, mx, my, :, cols] = total.astype(BF16)

    def up4(i):
        return (i + 4) % 4

    def one(h, i):
        return (up4(i), my) if h == 0 else (mx, up4(i))

    def span(s):
        return EXTRA // 2 if s == X else COLS

    def g1(s, h, i, start, width):
        x, y = one(h, i)
        if s == X:
            return extra.at[x, y, :, pl.ds(h * span(s) + start, width)]
        return rows.at[s, x, y, :, pl.ds(h * COLS + start, width)]

    def g4(s, h, j, start, width):
        cols = pl.ds(h * span(s) + start, width)
        if s == X:
            return extra.at[:, up4(j), :, cols] if h == 0 else extra.at[up4(j), :, :, cols]
        if h == 0:
            return rows.at[s, :, up4(j), :, cols]
        return rows.at[s, up4(j), :, :, cols]

    first, second = (mx, my), (my, mx)

    def dev1(h, step):
        return at(mx + step, my) if h == 0 else at(mx, my + step)

    def dev2(h, step):
        return at(mx, my + step) if h == 0 else at(mx + step, my)

    gathers = {}

    def gsend(s, h, k, ref, device):
        gathers[s, h, k] = send(ref, ref, ag_send.at[s, h, k], ag_recv.at[s, h, k], device)

    def gather1(s):
        for h in (0, 1):
            ref = g1(s, h, first[h], 0, span(s))
            gsend(s, h, 0, ref, dev1(h, 1))
            gsend(s, h, 1, ref, dev1(h, -1))

    def gather2(s):
        for h in (0, 1):
            gathers[s, h, 0].wait_recv()
            gsend(s, h, 2, g1(s, h, first[h] - 1, 0, span(s) // 2), dev1(h, 1))
            gathers[s, h, 1].wait_recv()
            gsend(s, h, 3, g1(s, h, first[h] + 1, span(s) // 2, span(s) // 2), dev1(h, -1))

    def gather3(s):
        for h in (0, 1):
            gathers[s, h, 2].wait_recv()
            gathers[s, h, 3].wait_recv()
            ref = g4(s, h, second[h], 0, span(s))
            gsend(s, h, 4, ref, dev2(h, 1))
            gsend(s, h, 5, ref, dev2(h, -1))

    def gather4(s):
        for h in (0, 1):
            gathers[s, h, 4].wait_recv()
            gsend(s, h, 6, g4(s, h, second[h] - 1, 0, span(s) // 2), dev2(h, 1))
            gathers[s, h, 5].wait_recv()
            gsend(s, h, 7, g4(s, h, second[h] + 1, span(s) // 2, span(s) // 2), dev2(h, -1))

    def gather5(s):
        for h in (0, 1):
            gathers[s, h, 6].wait_recv()
            gathers[s, h, 7].wait_recv()

    def gathered_out(s):
        for h in (0, 1):
            for k in range(8):
                gathers[s, h, k].wait_send()

    def pre_copy(s, i):
        return pltpu.make_async_remote_copy(
            src_ref=part.at[s, i],
            dst_ref=peer.at[s, i],
            send_sem=pre_send.at[s, i],
            recv_sem=pre_recv.at[s, i],
            device_id=pair,
            device_id_type=MESH,
        )

    last = (((1,), (1,)), ((), ()))
    lead = (((0,), (0,)), ((), ()))

    def partial_up(s):
        def step(i, carry):
            block = rows[s, i].reshape(4 * BLOCK, HALF)
            for u in (0, 1):
                value = jnp.dot(block, wu[u], preferred_element_type=F32)
                part[s, i, :, pl.ds(u * UNITS, UNITS)] = value.astype(BF16)
            pre_copy(s, i).start()
            return carry

        lax.fori_loop(0, 4, step, 0)

    def partial_back(s):
        def step(i, carry):
            block = rows[s, i].reshape(4 * BLOCK, HALF)
            for u in (0, 1):
                value = lax.dot_general(block, wd[u], last, preferred_element_type=F32)
                part[s, i, :, pl.ds(u * UNITS, UNITS)] = value.astype(BF16)
            pre_copy(s, i).start()
            return carry

        lax.fori_loop(0, 4, step, 0)

    def whole(s, i, u):
        here = part[s, i, :, pl.ds(u * UNITS, UNITS)].astype(F32)
        return here + peer[s, i, :, pl.ds((1 - u) * UNITS, UNITS)].astype(F32)

    def sigmoid(value):
        return 1.0 / (1.0 + jnp.exp(-value))

    def activate_back():
        def step(i, carry):
            pre_copy(B, i).wait_recv()
            pre_copy(B, i).wait_send()
            hidden, slope = [], []
            for u in (0, 1):
                pre = whole(B, i, u)
                gate = sigmoid(pre)
                hidden.append((pre * gate).astype(BF16))
                slope.append((gate * (1.0 + pre * (1.0 - gate))).astype(BF16))
            for u in (0, 1):
                peer[B, i, :, pl.ds(u * UNITS, UNITS)] = hidden[u]
                part[B, i, :, pl.ds(u * UNITS, UNITS)] = slope[u]
            return carry

        lax.fori_loop(0, 4, step, 0)

    def back_grad():
        def step(i, carry):
            pre_copy(G, i).wait_recv()
            value = []
            for u in (0, 1):
                slope = part[B, i, :, pl.ds(u * UNITS, UNITS)].astype(F32)
                value.append((whole(G, i, u) * slope).astype(BF16))
            for u in (0, 1):
                peer[G, i, :, pl.ds(u * UNITS, UNITS)] = value[u]
            return carry

        lax.fori_loop(0, 4, step, 0)

    def activate_fwd():
        def step(i, carry):
            pre_copy(F, i).wait_recv()
            hidden = []
            for u in (0, 1):
                pre = whole(F, i, u)
                hidden.append((pre * sigmoid(pre)).astype(BF16))
            for u in (0, 1):
                peer[F, i, :, pl.ds(u * UNITS, UNITS)] = hidden[u]
            return carry

        lax.fori_loop(0, 4, step, 0)

    def down_grad():
        for u, width in ((1, KEPT), (0, HALF)):
            def step(c, carry):
                cols = pl.ds(pl.multiple_of(c * TILE, TILE), TILE)
                left = peer[B, :, :, pl.ds(u * UNITS, UNITS)].reshape(16 * BLOCK, UNITS)
                right = rows[G, :, :, :, cols].reshape(16 * BLOCK, TILE)
                value = lax.dot_general(left, right, lead, preferred_element_type=F32)
                dgs[u, :, cols] = value.astype(BF16)
                return carry

            lax.fori_loop(0, width // TILE, step, 0)

    def down_grad_extra():
        def step(c, carry):
            start = pl.multiple_of(c * TILE, TILE)
            left = peer[B, :, :, pl.ds(0, UNITS)].reshape(16 * BLOCK, UNITS)
            right = extra[:, :, :, pl.ds(start, TILE)].reshape(16 * BLOCK, TILE)
            value = lax.dot_general(left, right, lead, preferred_element_type=F32)
            dgs[1, :, pl.ds(KEPT + start, TILE)] = value.astype(BF16)
            return carry

        lax.fori_loop(0, EXTRA // TILE, step, 0)

    def up_grad():
        def step(c, carry):
            cols = pl.ds(pl.multiple_of(c * TILE, TILE), TILE)
            left = rows[B, :, :, :, cols].reshape(16 * BLOCK, TILE)
            for u in (0, 1):
                right = peer[G, :, :, pl.ds(u * UNITS, UNITS)].reshape(16 * BLOCK, UNITS)
                value = lax.dot_general(left, right, lead, preferred_element_type=F32)
                ugs[u, cols, :] = value.astype(BF16)
            return carry

        lax.fori_loop(0, HALF // TILE, step, 0)

    def rows_out(s, source, weights, dims):
        def step(n, carry):
            i = n // (HALF // TILE)
            c = n % (HALF // TILE)
            cols = pl.ds(pl.multiple_of(c * TILE, TILE), TILE)
            total = None
            for u in (0, 1):
                left = peer[source, i, :, pl.ds(u * UNITS, UNITS)]
                right = weights[u, cols, :] if dims == last else weights[u, :, cols]
                if dims == last:
                    value = lax.dot_general(left, right, last, preferred_element_type=F32)
                else:
                    value = jnp.dot(left, right, preferred_element_type=F32)
                total = value if total is None else total + value
            rows[s, i, :, :, cols] = total.astype(BF16).reshape(4, BLOCK, TILE)
            return carry

        lax.fori_loop(0, 4 * (HALF // TILE), step, 0)

    scatters = {}

    def ssend(s, h, k, src, dst, device):
        scatters[s, h, k] = send(src, dst, rs_send.at[s - 1, h, k], rs_recv.at[s - 1, h, k], device)

    def add4(s, h, j, start, width, sources):
        cols = pl.ds(h * COLS + start, width)

        def step(i, carry):
            x, y = (i, up4(j)) if h == 0 else (up4(j), i)
            total = rows[s, x, y, :, cols].astype(F32)
            for source in sources:
                total += source[i].astype(F32)
            rows[s, x, y, :, cols] = total.astype(BF16)
            return carry

        lax.fori_loop(0, 4, step, 0)

    def sum1(s, h, i, start, width, sources):
        x, y = one(h, i)
        total = rows[s, x, y, :, pl.ds(h * COLS + start, width)].astype(F32)
        for source in sources:
            total += source[...].astype(F32)
        rows[s, x, y, :, pl.ds(h * COLS + start, width)] = total.astype(BF16)

    def scatter1(s):
        for h in (0, 1):
            far = second[h] + 2
            ssend(s, h, 0, g4(s, h, far, 0, QUARTER), r1.at[s - 1, h, 0], dev2(h, 1))
            ssend(s, h, 1, g4(s, h, far, QUARTER, QUARTER), r1.at[s - 1, h, 1], dev2(h, -1))

    def scatter2(s):
        for h in (0, 1):
            scatters[s, h, 0].wait_recv()
            add4(s, h, second[h] + 1, 0, QUARTER, [r1.at[s - 1, h, 0]])
            ssend(s, h, 2, g4(s, h, second[h] + 1, 0, COLS), r2.at[s - 1, h, 0], dev2(h, 1))
            scatters[s, h, 1].wait_recv()
            add4(s, h, second[h] - 1, QUARTER, QUARTER, [r1.at[s - 1, h, 1]])
            ssend(s, h, 3, g4(s, h, second[h] - 1, 0, COLS), r2.at[s - 1, h, 1], dev2(h, -1))

    def scatter3(s):
        for h in (0, 1):
            scatters[s, h, 2].wait_recv()
            scatters[s, h, 3].wait_recv()
            add4(s, h, second[h], 0, COLS, [r2.at[s - 1, h, 0], r2.at[s - 1, h, 1]])
            far = first[h] + 2
            ssend(s, h, 4, g1(s, h, far, 0, QUARTER), r3.at[s - 1, h, 0], dev1(h, 1))
            ssend(s, h, 5, g1(s, h, far, QUARTER, QUARTER), r3.at[s - 1, h, 1], dev1(h, -1))

    def scatter4(s):
        for h in (0, 1):
            scatters[s, h, 4].wait_recv()
            sum1(s, h, first[h] + 1, 0, QUARTER, [r3.at[s - 1, h, 0]])
            ssend(s, h, 6, g1(s, h, first[h] + 1, 0, COLS), r4.at[s - 1, h, 0], dev1(h, 1))
            scatters[s, h, 5].wait_recv()
            sum1(s, h, first[h] - 1, QUARTER, QUARTER, [r3.at[s - 1, h, 1]])
            ssend(s, h, 7, g1(s, h, first[h] - 1, 0, COLS), r4.at[s - 1, h, 1], dev1(h, -1))

    def scatter5(s, mine_ref, other_ref):
        for h in (0, 1):
            scatters[s, h, 6].wait_recv()
            scatters[s, h, 7].wait_recv()
            sum1(s, h, first[h], 0, COLS, [r4.at[s - 1, h, 0], r4.at[s - 1, h, 1]])
        for c in range(0, HALF, TILE):
            cols = pl.ds(c, TILE)
            block = rows[s, mx, my, :, cols]
            mine_ref[:, cols] = lax.dot_general(
                place_mine, block, lead, preferred_element_type=F32
            ).astype(BF16)
            other_ref[:, cols] = lax.dot_general(
                place_other, block, lead, preferred_element_type=F32
            ).astype(BF16)

    token[F] = pack(F, upper, order_f, active_f, weight_f)
    fetched[G] = fetch(xg_ref, upper, 0)
    token[B] = pack(B, lower, order_b, active_b, weight_b)
    wu_in.append(up_part(1))
    wu_own = keep(up_ref.at[mine], wu.at[0], 4)
    wd_own = keep(down_ref.at[:, mine], wd.at[0], 5)
    token[G] = pack(G, upper, order_b, active_b, weight_b)
    wu_in.append(up_part(2))
    wu_in.append(up_part(3))
    fill(F)
    gather1(F)
    gather2(F)
    gather3(F)
    wd_in = zsend(down_ref.at[:, other], wd.at[1], 4)
    fill(B)
    gather1(B)
    gather2(B)
    gather4(F)
    gather3(B)
    fill(G)
    gather1(G)
    gather5(F)
    fill_extra()
    for copy in wu_in:
        copy.wait_recv()
    wu_own.wait()
    partial_up(F)
    gather4(B)
    gather2(G)
    gather3(G)
    gather5(B)
    partial_up(B)
    gather4(G)
    activate_fwd()
    gathered_out(F)
    wd_in.wait_recv()
    wd_own.wait()
    rows_out(F, F, wd, None)
    scatter1(F)
    gather5(G)
    partial_back(G)
    scatter2(F)
    activate_back()
    gather1(X)
    down_grad()
    gather2(X)
    kept = pl.ds(pl.multiple_of(zh * HALF, HALF), KEPT)
    dg_out = zsend(dgs.at[1, :, pl.ds(0, KEPT)], dg_ref.at[:, kept], 5)
    dg_own = keep(dgs.at[0], dg_ref.at[:, mine], 6)
    gathered_out(G)
    scatter3(F)
    fin = zsend(xf_ref, fin_ref, 10, (after, me))
    told = zsend(info, info_ref, 3, (after, me))
    back_grad()
    rows_out(G, G, wu, last)
    gather3(X)
    scatter1(G)
    up_grad()
    ug_out = zsend(ugs.at[1], ug_ref.at[mine], 6)
    ug_own = keep(ugs.at[0], ug_ref.at[mine], 7)
    scatter4(F)
    scatter2(G)
    gather4(X)
    token[B].wait_send()
    token[G].wait_send()
    token[F].wait_send()
    token[X].wait_send()
    scatter5(F, local.at[2], remote.at[0])
    near_out = zsend(local.at[2], fout_ref.at[zh], 8, (after, me))
    far_out = zsend(remote.at[0], fout_ref.at[zh], 9, (after, mate))
    scatter3(G)
    gather5(X)
    down_grad_extra()
    far = pl.ds(pl.multiple_of((1 - zh) * HALF + KEPT, EXTRA), EXTRA)
    dg_far = keep(dgs.at[1, :, pl.ds(KEPT, EXTRA)], dg_ref.at[:, far], 9)
    scatter4(G)
    scatter5(G, local.at[0], local.at[1])
    row_own = keep(local.at[0], rout_ref.at[zh], 8)
    row_out = zsend(local.at[1], rout_ref.at[zh], 7)

    for copy in (dg_own, dg_far, ug_own, row_own):
        copy.wait()
    for copy in (dg_out, ug_out, row_out, near_out, far_out, fin, told):
        copy.wait()
    for copy in wu_in:
        copy.wait_send()
    wd_in.wait_send()
    gathered_out(B)
    gathered_out(X)
    for s in (G, F):
        for h in (0, 1):
            for k in range(8):
                scatters[s, h, k].wait_send()

    def done(n, carry):
        pre_copy(n // 4, n % 4).wait_send()
        return carry

    lax.fori_loop(4, 12, done, 0)


def relay(plans, xb, xg, xf, upper, lower):
    hbm = pl.BlockSpec(memory_space=pl.ANY)
    shapes = [
        jax.ShapeDtypeStruct(xf.shape, BF16),
        jax.ShapeDtypeStruct((2, SLOTS, HALF), BF16),
        jax.ShapeDtypeStruct((2, SLOTS, HALF), BF16),
        jax.ShapeDtypeStruct(upper.shape, BF16),
        jax.ShapeDtypeStruct(lower.shape, BF16),
        jax.ShapeDtypeStruct((8, TOKENS), F32),
    ]
    dma = pltpu.SemaphoreType.DMA
    return pl.pallas_call(
        kernel,
        out_shape=shapes,
        in_specs=[pl.BlockSpec(memory_space=pltpu.VMEM)] * 4 + [hbm] * 5,
        out_specs=[hbm] * 6,
        scratch_shapes=[
            pltpu.VMEM((8, TOKENS), F32),
            pltpu.VMEM((3, 4, 4, BLOCK, HALF), BF16),
            pltpu.VMEM((4, 4, BLOCK, EXTRA), BF16),
            pltpu.VMEM((SLOTS, EXTRA), BF16),
            pltpu.VMEM((SLOTS, EXTRA), BF16),
            pltpu.VMEM((2, HALF, UNITS), BF16),
            pltpu.VMEM((2, UNITS, HALF), BF16),
            pltpu.VMEM((3, SLOTS, HALF), BF16),
            pltpu.VMEM((3, SLOTS, HALF), BF16),
            pltpu.VMEM((3, 4, 4 * BLOCK, 2 * UNITS), BF16),
            pltpu.VMEM((3, 4, 4 * BLOCK, 2 * UNITS), BF16),
            pltpu.VMEM((2, UNITS, HALF), BF16),
            pltpu.VMEM((2, HALF, UNITS), BF16),
            pltpu.VMEM((2, 2, 2, 4, BLOCK, QUARTER), BF16),
            pltpu.VMEM((2, 2, 2, 4, BLOCK, COLS), BF16),
            pltpu.VMEM((2, 2, 2, BLOCK, QUARTER), BF16),
            pltpu.VMEM((2, 2, 2, BLOCK, COLS), BF16),
            dma((4, 2, 8)),
            dma((4, 2, 8)),
            dma((2, 2, 8)),
            dma((2, 2, 8)),
            dma((3, 4)),
            dma((3, 4)),
            dma((16,)),
            dma((16,)),
            dma((10,)),
        ],
        compiler_params=pltpu.CompilerParams(
            collective_id=0, has_side_effects=True, vmem_limit_bytes=64 * 1024 * 1024
        ),
        cost_estimate=pl.CostEstimate(
            flops=28_000_000_000, bytes_accessed=40_000_000, transcendentals=2_000_000
        ),
        name="relay",
    )(*plans, xb, xg, xf, upper, lower)


def column(line):
    down = lax.broadcasted_iota(jnp.int32, (TOKENS, TOKENS), 0)
    across = lax.broadcasted_iota(jnp.int32, (TOKENS, TOKENS), 1)
    return jnp.sum(jnp.where(down == across, line, 0.0), axis=1, keepdims=True)


def finish_kernel(
    ids_ref,
    shares_ref,
    info_ref,
    xg_ref,
    fin_ref,
    fout_ref,
    rout_ref,
    ug_ref,
    dg_ref,
    next_ref,
    grad_ref,
    up_ref,
    down_ref,
    xg,
    fin,
    fout,
    rout,
    up_held,
    down_held,
    row_sem,
    sem,
):
    halves = [pl.ds(half * HALF, HALF) for half in (0, 1)]

    def copy(src, dst, index, half):
        return pltpu.make_async_copy(src, dst, row_sem.at[index, half])

    row_loads = [
        [
            copy(fout_ref.at[half], fout.at[half], 0, half),
            copy(rout_ref.at[half], rout.at[half], 1, half),
            copy(fin_ref.at[:, halves[half]], fin.at[:, halves[half]], 2, half),
            copy(xg_ref.at[:, halves[half]], xg.at[:, halves[half]], 3, half),
        ]
        for half in (0, 1)
    ]
    row_stores = [
        [
            copy(fin.at[:, halves[half]], next_ref.at[:, halves[half]], 4, half),
            copy(xg.at[:, halves[half]], grad_ref.at[:, halves[half]], 5, half),
        ]
        for half in (0, 1)
    ]
    loads, stores = [], []
    for n in range(4):
        for k, (src, held, dst) in enumerate(((ug_ref, up_held, up_ref), (dg_ref, down_held, down_ref))):
            part = pl.ds(n * (src.shape[0] // 4), src.shape[0] // 4)
            loads.append(pltpu.make_async_copy(src.at[part], held.at[part], sem.at[0, k, n]))
            stores.append(pltpu.make_async_copy(held.at[part], dst.at[part], sem.at[1, k, n]))
    for load in row_loads[0] + loads[:4] + row_loads[1] + loads[4:]:
        load.start()
    expert = lax.axis_index("section")
    order, active, _ = route(ids_ref, shares_ref, expert)
    lead = (((0,), (0,)), ((), ()))
    place = lax.broadcasted_iota(jnp.int32, (SLOTS, TOKENS), 0).astype(F32)
    mine = jnp.where((order == place) & (active > 0.0), 1.0, 0.0).astype(BF16)
    theirs = jnp.where(info_ref[0:1, :] == place, 1.0, 0.0).astype(BF16)
    weight = column(info_ref[1:2, :])
    moves = iter(zip(loads, stores))
    for half in (0, 1):
        for load in row_loads[half]:
            load.wait()
        for c in range(0, HALF, TILE):
            here, there = pl.ds(c, TILE), pl.ds(half * HALF + c, TILE)
            spread = lax.dot_general(theirs, fout[half, :, here], lead, preferred_element_type=F32)
            fin[:, there] = (fin[:, there].astype(F32) + weight * spread).astype(BF16)
            spread = lax.dot_general(mine, rout[half, :, here], lead, preferred_element_type=F32)
            xg[:, there] = (xg[:, there].astype(F32) + spread).astype(BF16)
            load, store = next(moves)
            load.wait()
            store.start()
        for store in row_stores[half]:
            store.start()
    for store in stores + row_stores[0] + row_stores[1]:
        store.wait()


def finish(plan, info, xg, fin, fout, rout, up_grad, down_grad):
    hbm = pl.BlockSpec(memory_space=pl.ANY)
    vmem = pl.BlockSpec(memory_space=pltpu.VMEM)
    held = (xg, fin, fout, rout, up_grad, down_grad)
    return pl.pallas_call(
        finish_kernel,
        out_shape=[jax.ShapeDtypeStruct(a.shape, BF16) for a in (fin, xg, up_grad, down_grad)],
        in_specs=[vmem] * 3 + [hbm] * 6,
        out_specs=[hbm] * 4,
        scratch_shapes=[pltpu.VMEM(a.shape, BF16) for a in held]
        + [pltpu.SemaphoreType.DMA((6, 2)), pltpu.SemaphoreType.DMA((2, 2, 4))],
        compiler_params=pltpu.CompilerParams(vmem_limit_bytes=64 * 1024 * 1024),
        cost_estimate=pl.CostEstimate(
            flops=150_000_000, bytes_accessed=20_000_000, transcendentals=0
        ),
        name="finish",
    )(*plan, info, xg, fin, fout, rout, up_grad, down_grad)


def body(
    fwd_input,
    fwd_routes,
    fwd_weights,
    bwd_input,
    bwd_routes,
    bwd_weights,
    out_grad,
    up_weight,
    down_weight,
):
    plans = [fwd_routes[0].T, fwd_weights[0].T, bwd_routes[0].T, bwd_weights[0].T]
    fin, fout, rout, up_grad, down_grad, info = relay(
        plans, bwd_input[0], out_grad[0], fwd_input[0], up_weight[0], down_weight[0]
    )
    outs = finish(plans[2:], info, out_grad[0], fin, fout, rout, up_grad, down_grad)
    return tuple(out[None] for out in outs)


def solution(mesh):
    row_spec = P("section", "fsdp", None)
    in_specs = (row_spec,) * 7 + (P("section", None, "fsdp"), row_spec)
    out_specs = (row_spec, row_spec, P("section", None, "fsdp"), row_spec)
    return jax.shard_map(body, mesh=mesh, in_specs=in_specs, out_specs=out_specs, check_vma=False)
```

```python
import functools

import jax
import jax.numpy as jnp
from jax import lax
from jax.experimental import pallas as pl
from jax.experimental.pallas import tpu as pltpu
from jax.sharding import PartitionSpec as P

MESH = pl.DeviceIdType.MESH
F32 = jnp.float32
BF16 = jnp.bfloat16

CAP = 40
SLOTS = 48
D = 6144
HALF = D // 2
UNITS = 256
TOKENS = 128
BLOCK = 2 * CAP
COLS = HALF // 2
QUARTER = COLS // 2
TILE = 768
WIDE = 512

EXTRA = 1536
KEPT = HALF - EXTRA
B, G, F, X = 0, 1, 2, 3


def route(ids_ref, shares_ref, expert):
    hit = [ids_ref[pl.ds(k, 1), :] == expert for k in (0, 1)]
    share = [shares_ref[pl.ds(k, 1), :] for k in (0, 1)]
    active = jnp.where(hit[0] | hit[1], 1.0, 0.0)
    weight = jnp.where(hit[0], share[0], 0.0) + jnp.where(hit[1], share[1], 0.0)
    earlier = lax.broadcasted_iota(jnp.int32, (TOKENS, TOKENS), 0)
    later = lax.broadcasted_iota(jnp.int32, (TOKENS, TOKENS), 1)
    before = jnp.where(earlier < later, 1.0, 0.0).astype(BF16)
    spread = jnp.broadcast_to(active, (8, TOKENS)).astype(BF16)
    order = jnp.dot(spread, before, preferred_element_type=F32)[0:1]
    return order, active, weight


def kernel(
    ids_f_ref,
    shares_f_ref,
    ids_b_ref,
    shares_b_ref,
    xb_ref,
    xg_ref,
    xf_ref,
    up_ref,
    down_ref,
    fin_ref,
    fout_ref,
    rout_ref,
    ug_ref,
    dg_ref,
    info_ref,
    info,
    rows,
    extra,
    both,
    sent,
    got,
    wu,
    wd,
    local,
    remote,
    part,
    peer,
    dgs,
    r1,
    r2,
    r3,
    r4,
    ag_send,
    ag_recv,
    rs_send,
    rs_recv,
    pre_send,
    pre_recv,
    z_send,
    z_recv,
    loc_sem,
):
    sec = lax.axis_index("section")
    me = lax.axis_index("fsdp")
    mx = me // 8
    my = (me // 2) % 4
    zh = me % 2
    mate = me + 1 - 2 * zh
    after = (sec + 1) % 4
    before = (sec + 3) % 4

    def at(x, y):
        return (sec, (((x + 4) % 4) * 4 + (y + 4) % 4) * 2 + zh)

    pair = (sec, mate)

    barrier = pltpu.get_barrier_semaphore()
    near = [
        at(mx + 1, my),
        at(mx - 1, my),
        at(mx, my + 1),
        at(mx, my - 1),
        pair,
        (after, me),
        (after, mate),
        (before, me),
        (before, mate),
    ]
    for device in near:
        pl.semaphore_signal(barrier, inc=1, device_id=device, device_id_type=MESH)
    pl.semaphore_wait(barrier, len(near))

    mine = pl.ds(pl.multiple_of(zh * HALF, HALF), HALF)
    other = pl.ds(pl.multiple_of((1 - zh) * HALF, HALF), HALF)
    started = []

    def send(src, dst, send_sem, recv_sem, device):
        copy = pltpu.make_async_remote_copy(
            src_ref=src,
            dst_ref=dst,
            send_sem=send_sem,
            recv_sem=recv_sem,
            device_id=device,
            device_id_type=MESH,
        )
        copy.start()
        return copy

    def keep(src, dst, index):
        copy = pltpu.make_async_copy(src, dst, loc_sem.at[index])
        copy.start()
        return copy

    def zsend(src, dst, index, device=pair):
        return send(src, dst, z_send.at[index], z_recv.at[index], device)

    def up_part(n):
        width = HALF // 4
        start = pl.multiple_of((1 - zh) * HALF + n * width, width)
        return zsend(up_ref.at[pl.ds(start, width)], wu.at[1, pl.ds(n * width, width)], 11 + n)

    wu_in = [up_part(0)]
    upper, lower = pl.ds(0, TOKENS), pl.ds(TOKENS, TOKENS)

    def fetch(source, where, index):
        return [
            keep(source.at[:, pl.ds(half * HALF, HALF)], dgs.at[half, where], index + half)
            for half in (0, 1)
        ]

    fetched = {F: fetch(xf_ref, upper, 0), B: fetch(xb_ref, lower, 2)}

    token = {}

    def selector(order, active, count, offset):
        place = lax.broadcasted_iota(jnp.int32, (count, TOKENS), 0).astype(F32)
        return jnp.where((order + offset == place) & (active > 0.0), 1.0, 0.0)

    order_b, active_b, weight_b = route(ids_b_ref, shares_b_ref, sec)
    order_f, active_f, weight_f = route(ids_f_ref, shares_f_ref, sec)
    shift = (CAP * zh).astype(F32)
    line = lax.broadcasted_iota(jnp.int32, (8, TOKENS), 0)
    slots_f = jnp.where(active_f > 0.0, order_f, -1.0)
    info[...] = jnp.where(line == 0, slots_f, jnp.where(line == 1, weight_f, 0.0))

    slot = lax.broadcasted_iota(jnp.int32, (BLOCK, SLOTS), 1)
    row = lax.broadcasted_iota(jnp.int32, (BLOCK, SLOTS), 0)

    def place(which):
        hit = (row == slot + CAP * which) & (slot < CAP)
        return jnp.where(hit, 1.0, 0.0).astype(BF16)

    place_mine, place_other = place(zh), place(1 - zh)

    wide_slot = lax.broadcasted_iota(jnp.int32, (BLOCK, BLOCK), 1)
    wide_row = lax.broadcasted_iota(jnp.int32, (BLOCK, BLOCK), 0)

    def place_both(s, which):
        start = CAP if s == G else 0
        hit = (wide_row + start == wide_slot + CAP * which) & (wide_slot >= start)
        return jnp.where(hit & (wide_slot < start + CAP), 1.0, 0.0).astype(BF16)

    def pack(s, where, order, active, weight):
        for copy in fetched[s]:
            copy.wait()

        def rows_of(count, offset, half, start, width):
            chosen = selector(order, active, count, offset)
            value = jnp.dot(
                chosen.astype(BF16), dgs[half, where, pl.ds(start, width)], preferred_element_type=F32
            )
            if s == G:
                value = value * jnp.sum(chosen * weight, axis=1, keepdims=True)
            return value

        for c in range(0, HALF, TILE):
            cols = pl.ds(c, TILE)
            if s == F:
                local[s, :, cols] = rows_of(SLOTS, 0.0, 1 - zh, c, TILE).astype(BF16)
            elif s == B:
                both[0, :, cols] = rows_of(BLOCK, 0.0, 1 - zh, c, TILE).astype(BF16)
            else:
                total = both[0, :, cols].astype(F32)
                total += rows_of(BLOCK, float(CAP), 1 - zh, c, TILE)
                both[0, :, cols] = total.astype(BF16)
        if s == F:
            token[F] = zsend(local.at[F], remote.at[F], F)
        if s == G:
            token[G] = zsend(both.at[0], both.at[1], G)
            for c in range(0, EXTRA, WIDE):
                sent[:, pl.ds(c, WIDE)] = rows_of(SLOTS, 0.0, zh, KEPT + c, WIDE).astype(BF16)
            token[X] = zsend(sent, got, 15)
        for c in range(0, HALF, TILE):
            rows[s, mx, my, :, pl.ds(c, TILE)] = rows_of(BLOCK, shift, zh, c, TILE).astype(BF16)

    def fill_extra():
        token[X].wait_recv()
        for c in range(0, EXTRA, WIDE):
            cols = pl.ds(c, WIDE)
            total = jnp.dot(place_other, got[:, cols], preferred_element_type=F32)
            total += jnp.dot(
                place_both(G, zh), both[0, :, pl.ds(KEPT + c, WIDE)], preferred_element_type=F32
            )
            extra[mx, my, :, cols] = total.astype(BF16)

    def fill(s):
        if s != G:
            token[G if s == B else F].wait_recv()
        for c in range(0, HALF, TILE):
            cols = pl.ds(c, TILE)
            if s == F:
                total = jnp.dot(place_other, remote[s, :, cols], preferred_element_type=F32)
            else:
                total = jnp.dot(
                    place_both(s, 1 - zh), both[1, :, cols], preferred_element_type=F32
                )
            total += rows[s, mx, my, :, cols].astype(F32)
            rows[s, mx, my, :, cols] = total.astype(BF16)

    def up4(i):
        return (i + 4) % 4

    def one(h, i):
        return (up4(i), my) if h == 0 else (mx, up4(i))

    def span(s):
        return EXTRA // 2 if s == X else COLS

    def g1(s, h, i, start, width):
        x, y = one(h, i)
        if s == X:
            return extra.at[x, y, :, pl.ds(h * span(s) + start, width)]
        return rows.at[s, x, y, :, pl.ds(h * COLS + start, width)]

    def g4(s, h, j, start, width):
        cols = pl.ds(h * span(s) + start, width)
        if s == X:
            return extra.at[:, up4(j), :, cols] if h == 0 else extra.at[up4(j), :, :, cols]
        if h == 0:
            return rows.at[s, :, up4(j), :, cols]
        return rows.at[s, up4(j), :, :, cols]

    first, second = (mx, my), (my, mx)

    def dev1(h, step):
        return at(mx + step, my) if h == 0 else at(mx, my + step)

    def dev2(h, step):
        return at(mx, my + step) if h == 0 else at(mx + step, my)

    gathers = {}

    def gsend(s, h, k, ref, device):
        gathers[s, h, k] = send(ref, ref, ag_send.at[s, h, k], ag_recv.at[s, h, k], device)

    def gather1(s):
        for h in (0, 1):
            ref = g1(s, h, first[h], 0, span(s))
            gsend(s, h, 0, ref, dev1(h, 1))
            gsend(s, h, 1, ref, dev1(h, -1))

    def gather2(s):
        for h in (0, 1):
            gathers[s, h, 0].wait_recv()
            gsend(s, h, 2, g1(s, h, first[h] - 1, 0, span(s) // 2), dev1(h, 1))
            gathers[s, h, 1].wait_recv()
            gsend(s, h, 3, g1(s, h, first[h] + 1, span(s) // 2, span(s) // 2), dev1(h, -1))

    def gather3(s):
        for h in (0, 1):
            gathers[s, h, 2].wait_recv()
            gathers[s, h, 3].wait_recv()
            ref = g4(s, h, second[h], 0, span(s))
            gsend(s, h, 4, ref, dev2(h, 1))
            gsend(s, h, 5, ref, dev2(h, -1))

    def gather4(s):
        for h in (0, 1):
            gathers[s, h, 4].wait_recv()
            gsend(s, h, 6, g4(s, h, second[h] - 1, 0, span(s) // 2), dev2(h, 1))
            gathers[s, h, 5].wait_recv()
            gsend(s, h, 7, g4(s, h, second[h] + 1, span(s) // 2, span(s) // 2), dev2(h, -1))

    def gather5(s):
        for h in (0, 1):
            gathers[s, h, 6].wait_recv()
            gathers[s, h, 7].wait_recv()

    def gathered_out(s):
        for h in (0, 1):
            for k in range(8):
                gathers[s, h, k].wait_send()

    def pre_copy(s, i):
        return pltpu.make_async_remote_copy(
            src_ref=part.at[s, i],
            dst_ref=peer.at[s, i],
            send_sem=pre_send.at[s, i],
            recv_sem=pre_recv.at[s, i],
            device_id=pair,
            device_id_type=MESH,
        )

    last = (((1,), (1,)), ((), ()))
    lead = (((0,), (0,)), ((), ()))

    def turn(n):
        return (mx + 2 + n) % 4

    def partial_up(s):
        def step(n, carry):
            i = turn(n)
            block = rows[s, i].reshape(4 * BLOCK, HALF)
            for u in (0, 1):
                value = jnp.dot(block, wu[u], preferred_element_type=F32)
                part[s, i, :, pl.ds(u * UNITS, UNITS)] = value.astype(BF16)
            pre_copy(s, i).start()
            return carry

        lax.fori_loop(0, 4, step, 0)

    def partial_back(s):
        def step(n, carry):
            i = turn(n)
            block = rows[s, i].reshape(4 * BLOCK, HALF)
            for u in (0, 1):
                value = lax.dot_general(block, wd[u], last, preferred_element_type=F32)
                part[s, i, :, pl.ds(u * UNITS, UNITS)] = value.astype(BF16)
            pre_copy(s, i).start()
            return carry

        lax.fori_loop(0, 4, step, 0)

    def whole(s, i, u):
        here = part[s, i, :, pl.ds(u * UNITS, UNITS)].astype(F32)
        return here + peer[s, i, :, pl.ds((1 - u) * UNITS, UNITS)].astype(F32)

    def sigmoid(value):
        return 1.0 / (1.0 + jnp.exp(-value))

    def activate_back():
        def step(i, carry):
            pre_copy(B, i).wait_recv()
            pre_copy(B, i).wait_send()
            hidden, slope = [], []
            for u in (0, 1):
                pre = whole(B, i, u)
                gate = sigmoid(pre)
                hidden.append((pre * gate).astype(BF16))
                slope.append((gate * (1.0 + pre * (1.0 - gate))).astype(BF16))
            for u in (0, 1):
                peer[B, i, :, pl.ds(u * UNITS, UNITS)] = hidden[u]
                part[B, i, :, pl.ds(u * UNITS, UNITS)] = slope[u]
            return carry

        lax.fori_loop(0, 4, step, 0)

    def back_grad(i):
        pre_copy(G, i).wait_recv()
        value = []
        for u in (0, 1):
            slope = part[B, i, :, pl.ds(u * UNITS, UNITS)].astype(F32)
            value.append((whole(G, i, u) * slope).astype(BF16))
        for u in (0, 1):
            peer[G, i, :, pl.ds(u * UNITS, UNITS)] = value[u]

    def activate_fwd(i):
        pre_copy(F, i).wait_recv()
        hidden = []
        for u in (0, 1):
            pre = whole(F, i, u)
            hidden.append((pre * sigmoid(pre)).astype(BF16))
        for u in (0, 1):
            peer[F, i, :, pl.ds(u * UNITS, UNITS)] = hidden[u]

    def down_grad():
        for u, width in ((1, KEPT), (0, HALF)):
            def step(c, carry):
                cols = pl.ds(pl.multiple_of(c * WIDE, WIDE), WIDE)
                left = peer[B, :, :, pl.ds(u * UNITS, UNITS)].reshape(16 * BLOCK, UNITS)
                right = rows[G, :, :, :, cols].reshape(16 * BLOCK, WIDE)
                value = lax.dot_general(left, right, lead, preferred_element_type=F32)
                dgs[u, :, cols] = value.astype(BF16)
                return carry

            lax.fori_loop(0, width // WIDE, step, 0)

    def down_grad_extra():
        def step(c, carry):
            start = pl.multiple_of(c * WIDE, WIDE)
            left = peer[B, :, :, pl.ds(0, UNITS)].reshape(16 * BLOCK, UNITS)
            right = extra[:, :, :, pl.ds(start, WIDE)].reshape(16 * BLOCK, WIDE)
            value = lax.dot_general(left, right, lead, preferred_element_type=F32)
            dgs[1, :, pl.ds(KEPT + start, WIDE)] = value.astype(BF16)
            return carry

        lax.fori_loop(0, EXTRA // WIDE, step, 0)

    def up_grad():
        def step(c, carry):
            cols = pl.ds(pl.multiple_of(c * TILE, TILE), TILE)
            left = rows[B, :, :, :, cols].reshape(16 * BLOCK, TILE)
            for u in (0, 1):
                right = peer[G, :, :, pl.ds(u * UNITS, UNITS)].reshape(16 * BLOCK, UNITS)
                value = lax.dot_general(left, right, lead, preferred_element_type=F32)
                wu[u, cols, :] = value.astype(BF16)
            return carry

        lax.fori_loop(0, HALF // TILE, step, 0)

    def rows_out(s, activate, weights, dims):
        def column(n, carry):
            i = turn(n)
            activate(i)

            def step(c, carry):
                cols = pl.ds(pl.multiple_of(c * TILE, TILE), TILE)
                total = None
                for u in (0, 1):
                    left = peer[s, i, :, pl.ds(u * UNITS, UNITS)]
                    right = weights[u, cols, :] if dims == last else weights[u, :, cols]
                    if dims == last:
                        value = lax.dot_general(left, right, last, preferred_element_type=F32)
                    else:
                        value = jnp.dot(left, right, preferred_element_type=F32)
                    total = value if total is None else total + value
                rows[s, i, :, :, cols] = total.astype(BF16).reshape(4, BLOCK, TILE)
                return carry

            lax.fori_loop(0, HALF // TILE, step, 0)
            return carry

        lax.fori_loop(0, 1, column, 0)
        scatter1(s, 1)
        lax.fori_loop(1, 4, column, 0)
        scatter1(s, 0)

    scatters = {}

    def ssend(s, h, k, src, dst, device):
        scatters[s, h, k] = send(src, dst, rs_send.at[s - 1, h, k], rs_recv.at[s - 1, h, k], device)

    def add4(s, h, j, start, width, sources):
        cols = pl.ds(h * COLS + start, width)

        def step(i, carry):
            x, y = (i, up4(j)) if h == 0 else (up4(j), i)
            total = rows[s, x, y, :, cols].astype(F32)
            for source in sources:
                total += source[i].astype(F32)
            rows[s, x, y, :, cols] = total.astype(BF16)
            return carry

        lax.fori_loop(0, 4, step, 0)

    def sum1(s, h, i, start, width, sources):
        x, y = one(h, i)
        total = rows[s, x, y, :, pl.ds(h * COLS + start, width)].astype(F32)
        for source in sources:
            total += source[...].astype(F32)
        rows[s, x, y, :, pl.ds(h * COLS + start, width)] = total.astype(BF16)

    def scatter1(s, h):
        far = second[h] + 2
        ssend(s, h, 0, g4(s, h, far, 0, QUARTER), r1.at[s - 1, h, 0], dev2(h, 1))
        ssend(s, h, 1, g4(s, h, far, QUARTER, QUARTER), r1.at[s - 1, h, 1], dev2(h, -1))

    def scatter2(s):
        for h in (1, 0):
            scatters[s, h, 0].wait_recv()
            add4(s, h, second[h] + 1, 0, QUARTER, [r1.at[s - 1, h, 0]])
            ssend(s, h, 2, g4(s, h, second[h] + 1, 0, COLS), r2.at[s - 1, h, 0], dev2(h, 1))
            scatters[s, h, 1].wait_recv()
            add4(s, h, second[h] - 1, QUARTER, QUARTER, [r1.at[s - 1, h, 1]])
            ssend(s, h, 3, g4(s, h, second[h] - 1, 0, COLS), r2.at[s - 1, h, 1], dev2(h, -1))

    def scatter3(s):
        for h in (0, 1):
            scatters[s, h, 2].wait_recv()
            scatters[s, h, 3].wait_recv()
            add4(s, h, second[h], 0, COLS, [r2.at[s - 1, h, 0], r2.at[s - 1, h, 1]])
            far = first[h] + 2
            ssend(s, h, 4, g1(s, h, far, 0, QUARTER), r3.at[s - 1, h, 0], dev1(h, 1))
            ssend(s, h, 5, g1(s, h, far, QUARTER, QUARTER), r3.at[s - 1, h, 1], dev1(h, -1))

    def scatter4(s):
        for h in (0, 1):
            scatters[s, h, 4].wait_recv()
            sum1(s, h, first[h] + 1, 0, QUARTER, [r3.at[s - 1, h, 0]])
            ssend(s, h, 6, g1(s, h, first[h] + 1, 0, COLS), r4.at[s - 1, h, 0], dev1(h, 1))
            scatters[s, h, 5].wait_recv()
            sum1(s, h, first[h] - 1, QUARTER, QUARTER, [r3.at[s - 1, h, 1]])
            ssend(s, h, 7, g1(s, h, first[h] - 1, 0, COLS), r4.at[s - 1, h, 1], dev1(h, -1))

    def scatter5(s, mine_ref, other_ref):
        for h in (0, 1):
            scatters[s, h, 6].wait_recv()
            scatters[s, h, 7].wait_recv()
            sum1(s, h, first[h], 0, COLS, [r4.at[s - 1, h, 0], r4.at[s - 1, h, 1]])
        for c in range(0, HALF, TILE):
            cols = pl.ds(c, TILE)
            block = rows[s, mx, my, :, cols]
            mine_ref[:, cols] = lax.dot_general(
                place_mine, block, lead, preferred_element_type=F32
            ).astype(BF16)
            other_ref[:, cols] = lax.dot_general(
                place_other, block, lead, preferred_element_type=F32
            ).astype(BF16)

    pack(F, upper, order_f, active_f, weight_f)
    fetched[G] = fetch(xg_ref, upper, 0)
    pack(B, lower, order_b, active_b, weight_b)
    wu_in.append(up_part(1))
    wu_own = keep(up_ref.at[mine], wu.at[0], 4)
    wd_own = keep(down_ref.at[:, mine], wd.at[0], 5)
    pack(G, upper, order_b, active_b, weight_b)
    wu_in.append(up_part(2))
    wu_in.append(up_part(3))
    fill(F)
    gather1(F)
    gather2(F)
    gather3(F)
    wd_in = zsend(down_ref.at[:, other], wd.at[1], 4)
    fill(B)
    gather1(B)
    gather2(B)
    gather4(F)
    gather3(B)
    fill(G)
    gather1(G)
    gather5(F)
    fill_extra()
    for copy in wu_in:
        copy.wait_recv()
    wu_own.wait()
    partial_up(F)
    gather4(B)
    gather2(G)
    gather3(G)
    gather5(B)
    partial_up(B)
    gather4(G)
    gathered_out(F)
    wd_in.wait_recv()
    wd_own.wait()
    rows_out(F, activate_fwd, wd, None)
    gather5(G)
    partial_back(G)
    scatter2(F)
    fin = zsend(xf_ref, fin_ref, 10, (after, me))
    activate_back()
    gather1(X)
    down_grad()
    gather2(X)
    kept = pl.ds(pl.multiple_of(zh * HALF, HALF), KEPT)
    dg_out = zsend(dgs.at[1, :, pl.ds(0, KEPT)], dg_ref.at[:, kept], 5)
    dg_own = keep(dgs.at[0], dg_ref.at[:, mine], 6)
    gathered_out(G)
    scatter3(F)
    told = zsend(info, info_ref, 3, (after, me))
    rows_out(G, back_grad, wu, last)
    gather3(X)
    up_grad()
    ug_out = zsend(wu.at[1], ug_ref.at[mine], 6)
    ug_own = keep(wu.at[0], ug_ref.at[mine], 7)
    scatter2(G)
    scatter4(F)
    gather4(X)
    token[G].wait_send()
    token[F].wait_send()
    token[X].wait_send()
    scatter5(F, local.at[2], remote.at[0])
    near_out = zsend(local.at[2], fout_ref.at[zh], 8, (after, me))
    far_out = zsend(remote.at[0], fout_ref.at[zh], 9, (after, mate))
    scatter3(G)
    scatter4(G)
    scatter5(G, local.at[0], local.at[1])
    row_own = keep(local.at[0], rout_ref.at[zh], 8)
    row_out = zsend(local.at[1], rout_ref.at[zh], 7)
    gather5(X)
    down_grad_extra()
    far = pl.ds(pl.multiple_of((1 - zh) * HALF + KEPT, WIDE), EXTRA)
    dg_far = keep(dgs.at[1, :, pl.ds(KEPT, EXTRA)], dg_ref.at[:, far], 9)

    for copy in (dg_own, dg_far, ug_own, row_own):
        copy.wait()
    for copy in (dg_out, ug_out, row_out, near_out, far_out, fin, told):
        copy.wait()
    for copy in wu_in:
        copy.wait_send()
    wd_in.wait_send()
    gathered_out(B)
    gathered_out(X)
    for s in (G, F):
        for h in (0, 1):
            for k in range(8):
                scatters[s, h, k].wait_send()

    def done(n, carry):
        pre_copy(n // 4, n % 4).wait_send()
        return carry

    lax.fori_loop(4, 12, done, 0)


def relay(plans, xb, xg, xf, upper, lower):
    hbm = pl.BlockSpec(memory_space=pl.ANY)
    shapes = [
        jax.ShapeDtypeStruct(xf.shape, BF16),
        jax.ShapeDtypeStruct((2, SLOTS, HALF), BF16),
        jax.ShapeDtypeStruct((2, SLOTS, HALF), BF16),
        jax.ShapeDtypeStruct(upper.shape, BF16),
        jax.ShapeDtypeStruct(lower.shape, BF16),
        jax.ShapeDtypeStruct((8, TOKENS), F32),
    ]
    dma = pltpu.SemaphoreType.DMA
    return pl.pallas_call(
        kernel,
        out_shape=shapes,
        in_specs=[pl.BlockSpec(memory_space=pltpu.VMEM)] * 4 + [hbm] * 5,
        out_specs=[hbm] * 6,
        scratch_shapes=[
            pltpu.VMEM((8, TOKENS), F32),
            pltpu.VMEM((3, 4, 4, BLOCK, HALF), BF16),
            pltpu.VMEM((4, 4, BLOCK, EXTRA), BF16),
            pltpu.VMEM((2, BLOCK, HALF), BF16),
            pltpu.VMEM((SLOTS, EXTRA), BF16),
            pltpu.VMEM((SLOTS, EXTRA), BF16),
            pltpu.VMEM((2, HALF, UNITS), BF16),
            pltpu.VMEM((2, UNITS, HALF), BF16),
            pltpu.VMEM((3, SLOTS, HALF), BF16),
            pltpu.VMEM((3, SLOTS, HALF), BF16),
            pltpu.VMEM((3, 4, 4 * BLOCK, 2 * UNITS), BF16),
            pltpu.VMEM((3, 4, 4 * BLOCK, 2 * UNITS), BF16),
            pltpu.VMEM((2, UNITS, HALF), BF16),
            pltpu.VMEM((2, 2, 2, 4, BLOCK, QUARTER), BF16),
            pltpu.VMEM((2, 2, 2, 4, BLOCK, COLS), BF16),
            pltpu.VMEM((2, 2, 2, BLOCK, QUARTER), BF16),
            pltpu.VMEM((2, 2, 2, BLOCK, COLS), BF16),
            dma((4, 2, 8)),
            dma((4, 2, 8)),
            dma((2, 2, 8)),
            dma((2, 2, 8)),
            dma((3, 4)),
            dma((3, 4)),
            dma((16,)),
            dma((16,)),
            dma((10,)),
        ],
        compiler_params=pltpu.CompilerParams(
            collective_id=0, has_side_effects=True, vmem_limit_bytes=64 * 1024 * 1024
        ),
        cost_estimate=pl.CostEstimate(
            flops=28_000_000_000, bytes_accessed=40_000_000, transcendentals=2_000_000
        ),
        name="relay",
    )(*plans, xb, xg, xf, upper, lower)


def column(line):
    down = lax.broadcasted_iota(jnp.int32, (TOKENS, TOKENS), 0)
    across = lax.broadcasted_iota(jnp.int32, (TOKENS, TOKENS), 1)
    return jnp.sum(jnp.where(down == across, line, 0.0), axis=1, keepdims=True)


def finish_kernel(
    ids_ref,
    shares_ref,
    info_ref,
    xg_ref,
    fin_ref,
    fout_ref,
    rout_ref,
    ug_ref,
    dg_ref,
    next_ref,
    grad_ref,
    up_ref,
    down_ref,
    xg,
    fin,
    fout,
    rout,
    up_held,
    down_held,
    row_sem,
    sem,
):
    halves = [pl.ds(half * HALF, HALF) for half in (0, 1)]

    def copy(src, dst, index, half):
        return pltpu.make_async_copy(src, dst, row_sem.at[index, half])

    row_loads = [
        [
            copy(fout_ref.at[half], fout.at[half], 0, half),
            copy(rout_ref.at[half], rout.at[half], 1, half),
            copy(fin_ref.at[:, halves[half]], fin.at[:, halves[half]], 2, half),
            copy(xg_ref.at[:, halves[half]], xg.at[:, halves[half]], 3, half),
        ]
        for half in (0, 1)
    ]
    row_stores = [
        [
            copy(fin.at[:, halves[half]], next_ref.at[:, halves[half]], 4, half),
            copy(xg.at[:, halves[half]], grad_ref.at[:, halves[half]], 5, half),
        ]
        for half in (0, 1)
    ]
    loads, stores = [], []
    for n in range(4):
        for k, (src, held, dst) in enumerate(((ug_ref, up_held, up_ref), (dg_ref, down_held, down_ref))):
            part = pl.ds(n * (src.shape[0] // 4), src.shape[0] // 4)
            loads.append(pltpu.make_async_copy(src.at[part], held.at[part], sem.at[0, k, n]))
            stores.append(pltpu.make_async_copy(held.at[part], dst.at[part], sem.at[1, k, n]))
    for load in row_loads[0] + loads[:4] + row_loads[1] + loads[4:]:
        load.start()
    expert = lax.axis_index("section")
    order, active, _ = route(ids_ref, shares_ref, expert)
    lead = (((0,), (0,)), ((), ()))
    place = lax.broadcasted_iota(jnp.int32, (SLOTS, TOKENS), 0).astype(F32)
    mine = jnp.where((order == place) & (active > 0.0), 1.0, 0.0).astype(BF16)
    theirs = jnp.where(info_ref[0:1, :] == place, 1.0, 0.0).astype(BF16)
    weight = column(info_ref[1:2, :])
    moves = iter(zip(loads, stores))
    for half in (0, 1):
        for load in row_loads[half]:
            load.wait()
        for c in range(0, HALF, TILE):
            here, there = pl.ds(c, TILE), pl.ds(half * HALF + c, TILE)
            spread = lax.dot_general(theirs, fout[half, :, here], lead, preferred_element_type=F32)
            fin[:, there] = (fin[:, there].astype(F32) + weight * spread).astype(BF16)
            spread = lax.dot_general(mine, rout[half, :, here], lead, preferred_element_type=F32)
            xg[:, there] = (xg[:, there].astype(F32) + spread).astype(BF16)
            load, store = next(moves)
            load.wait()
            store.start()
        for store in row_stores[half]:
            store.start()
    for store in stores + row_stores[0] + row_stores[1]:
        store.wait()


def finish(plan, info, xg, fin, fout, rout, up_grad, down_grad):
    hbm = pl.BlockSpec(memory_space=pl.ANY)
    vmem = pl.BlockSpec(memory_space=pltpu.VMEM)
    held = (xg, fin, fout, rout, up_grad, down_grad)
    return pl.pallas_call(
        finish_kernel,
        out_shape=[jax.ShapeDtypeStruct(a.shape, BF16) for a in (fin, xg, up_grad, down_grad)],
        in_specs=[vmem] * 3 + [hbm] * 6,
        out_specs=[hbm] * 4,
        scratch_shapes=[pltpu.VMEM(a.shape, BF16) for a in held]
        + [pltpu.SemaphoreType.DMA((6, 2)), pltpu.SemaphoreType.DMA((2, 2, 4))],
        compiler_params=pltpu.CompilerParams(vmem_limit_bytes=64 * 1024 * 1024),
        cost_estimate=pl.CostEstimate(
            flops=150_000_000, bytes_accessed=20_000_000, transcendentals=0
        ),
        name="finish",
    )(*plan, info, xg, fin, fout, rout, up_grad, down_grad)


def body(
    fwd_input,
    fwd_routes,
    fwd_weights,
    bwd_input,
    bwd_routes,
    bwd_weights,
    out_grad,
    up_weight,
    down_weight,
):
    plans = [fwd_routes[0].T, fwd_weights[0].T, bwd_routes[0].T, bwd_weights[0].T]
    fin, fout, rout, up_grad, down_grad, info = relay(
        plans, bwd_input[0], out_grad[0], fwd_input[0], up_weight[0], down_weight[0]
    )
    outs = finish(plans[2:], info, out_grad[0], fin, fout, rout, up_grad, down_grad)
    return tuple(out[None] for out in outs)


def solution(mesh):
    row_spec = P("section", "fsdp", None)
    in_specs = (row_spec,) * 7 + (P("section", None, "fsdp"), row_spec)
    out_specs = (row_spec, row_spec, P("section", None, "fsdp"), row_spec)
    return jax.shard_map(body, mesh=mesh, in_specs=in_specs, out_specs=out_specs, check_vma=False)
```

```python
import functools

import jax
import jax.numpy as jnp
from jax import lax
from jax.experimental import pallas as pl
from jax.experimental.pallas import tpu as pltpu
from jax.sharding import PartitionSpec as P

MESH = pl.DeviceIdType.MESH
F32 = jnp.float32
BF16 = jnp.bfloat16

CAP = 40
SLOTS = 48
D = 6144
HALF = D // 2
UNITS = 256
TOKENS = 128
BLOCK = 2 * CAP
COLS = HALF // 2
QUARTER = COLS // 2
TILE = 768
WIDE = 512

EXTRA = 1536
KEPT = HALF - EXTRA
B, G, F, X = 0, 1, 2, 3


def route(ids_ref, shares_ref, expert):
    hit = [ids_ref[pl.ds(k, 1), :] == expert for k in (0, 1)]
    share = [shares_ref[pl.ds(k, 1), :] for k in (0, 1)]
    active = jnp.where(hit[0] | hit[1], 1.0, 0.0)
    weight = jnp.where(hit[0], share[0], 0.0) + jnp.where(hit[1], share[1], 0.0)
    earlier = lax.broadcasted_iota(jnp.int32, (TOKENS, TOKENS), 0)
    later = lax.broadcasted_iota(jnp.int32, (TOKENS, TOKENS), 1)
    before = jnp.where(earlier < later, 1.0, 0.0).astype(BF16)
    spread = jnp.broadcast_to(active, (8, TOKENS)).astype(BF16)
    order = jnp.dot(spread, before, preferred_element_type=F32)[0:1]
    return order, active, weight


def kernel(
    ids_f_ref,
    shares_f_ref,
    ids_b_ref,
    shares_b_ref,
    xb_ref,
    xg_ref,
    xf_ref,
    up_ref,
    down_ref,
    fin_ref,
    fout_ref,
    rout_ref,
    ug_ref,
    dg_ref,
    info_ref,
    info,
    rows,
    extra,
    both,
    sent,
    got,
    wu,
    wd,
    local,
    remote,
    part,
    peer,
    dgs,
    r1,
    r2,
    r3,
    r4,
    ag_send,
    ag_recv,
    rs_send,
    rs_recv,
    pre_send,
    pre_recv,
    z_send,
    z_recv,
    loc_sem,
):
    sec = lax.axis_index("section")
    me = lax.axis_index("fsdp")
    mx = me // 8
    my = (me // 2) % 4
    zh = me % 2
    mate = me + 1 - 2 * zh
    after = (sec + 1) % 4
    before = (sec + 3) % 4

    def at(x, y):
        return (sec, (((x + 4) % 4) * 4 + (y + 4) % 4) * 2 + zh)

    pair = (sec, mate)

    barrier = pltpu.get_barrier_semaphore()
    near = [
        at(mx + 1, my),
        at(mx - 1, my),
        at(mx, my + 1),
        at(mx, my - 1),
        pair,
        (after, me),
        (after, mate),
        (before, me),
        (before, mate),
    ]
    for device in near:
        pl.semaphore_signal(barrier, inc=1, device_id=device, device_id_type=MESH)
    pl.semaphore_wait(barrier, len(near))

    mine = pl.ds(pl.multiple_of(zh * HALF, HALF), HALF)
    other = pl.ds(pl.multiple_of((1 - zh) * HALF, HALF), HALF)
    started = []

    def send(src, dst, send_sem, recv_sem, device):
        copy = pltpu.make_async_remote_copy(
            src_ref=src,
            dst_ref=dst,
            send_sem=send_sem,
            recv_sem=recv_sem,
            device_id=device,
            device_id_type=MESH,
        )
        copy.start()
        return copy

    def keep(src, dst, index):
        copy = pltpu.make_async_copy(src, dst, loc_sem.at[index])
        copy.start()
        return copy

    def zsend(src, dst, index, device=pair):
        return send(src, dst, z_send.at[index], z_recv.at[index], device)

    def up_part(n):
        width = HALF // 4
        start = pl.multiple_of((1 - zh) * HALF + n * width, width)
        return zsend(up_ref.at[pl.ds(start, width)], wu.at[1, pl.ds(n * width, width)], 11 + n)

    wu_in = [up_part(0)]
    upper, lower = pl.ds(0, TOKENS), pl.ds(TOKENS, TOKENS)

    def fetch(source, where, index):
        return [
            keep(source.at[:, pl.ds(half * HALF, HALF)], dgs.at[half, where], index + half)
            for half in (0, 1)
        ]

    fetched = {F: fetch(xf_ref, upper, 0), B: fetch(xb_ref, lower, 2)}

    token = {}

    def selector(order, active, count, offset):
        place = lax.broadcasted_iota(jnp.int32, (count, TOKENS), 0).astype(F32)
        return jnp.where((order + offset == place) & (active > 0.0), 1.0, 0.0)

    order_b, active_b, weight_b = route(ids_b_ref, shares_b_ref, sec)
    order_f, active_f, weight_f = route(ids_f_ref, shares_f_ref, sec)
    shift = (CAP * zh).astype(F32)
    line = lax.broadcasted_iota(jnp.int32, (8, TOKENS), 0)
    slots_f = jnp.where(active_f > 0.0, order_f, -1.0)
    info[...] = jnp.where(line == 0, slots_f, jnp.where(line == 1, weight_f, 0.0))

    slot = lax.broadcasted_iota(jnp.int32, (BLOCK, SLOTS), 1)
    row = lax.broadcasted_iota(jnp.int32, (BLOCK, SLOTS), 0)

    def place(which):
        hit = (row == slot + CAP * which) & (slot < CAP)
        return jnp.where(hit, 1.0, 0.0).astype(BF16)

    place_mine, place_other = place(zh), place(1 - zh)

    wide_slot = lax.broadcasted_iota(jnp.int32, (BLOCK, BLOCK), 1)
    wide_row = lax.broadcasted_iota(jnp.int32, (BLOCK, BLOCK), 0)

    def place_both(s, which):
        start = CAP if s == G else 0
        hit = (wide_row + start == wide_slot + CAP * which) & (wide_slot >= start)
        return jnp.where(hit & (wide_slot < start + CAP), 1.0, 0.0).astype(BF16)

    def pack(s, where, order, active, weight):
        for copy in fetched[s]:
            copy.wait()

        def rows_of(count, offset, half, start, width):
            chosen = selector(order, active, count, offset)
            value = jnp.dot(
                chosen.astype(BF16), dgs[half, where, pl.ds(start, width)], preferred_element_type=F32
            )
            if s == G:
                value = value * jnp.sum(chosen * weight, axis=1, keepdims=True)
            return value

        for c in range(0, HALF, TILE):
            cols = pl.ds(c, TILE)
            if s == F:
                local[s, :, cols] = rows_of(SLOTS, 0.0, 1 - zh, c, TILE).astype(BF16)
            elif s == B:
                both[0, :, cols] = rows_of(BLOCK, 0.0, 1 - zh, c, TILE).astype(BF16)
            else:
                total = both[0, :, cols].astype(F32)
                total += rows_of(BLOCK, float(CAP), 1 - zh, c, TILE)
                both[0, :, cols] = total.astype(BF16)
        if s == F:
            token[F] = zsend(local.at[F], remote.at[F], F)
        if s == G:
            token[G] = zsend(both.at[0], both.at[1], G)
            for c in range(0, EXTRA, WIDE):
                sent[:, pl.ds(c, WIDE)] = rows_of(SLOTS, 0.0, zh, KEPT + c, WIDE).astype(BF16)
            token[X] = zsend(sent, got, 15)
        for c in range(0, HALF, TILE):
            rows[s, mx, my, :, pl.ds(c, TILE)] = rows_of(BLOCK, shift, zh, c, TILE).astype(BF16)

    def fill_extra():
        token[X].wait_recv()
        for c in range(0, EXTRA, WIDE):
            cols = pl.ds(c, WIDE)
            total = jnp.dot(place_other, got[:, cols], preferred_element_type=F32)
            total += jnp.dot(
                place_both(G, zh), both[0, :, pl.ds(KEPT + c, WIDE)], preferred_element_type=F32
            )
            extra[mx, my, :, cols] = total.astype(BF16)

    def fill(s):
        if s != G:
            token[G if s == B else F].wait_recv()
        for c in range(0, HALF, TILE):
            cols = pl.ds(c, TILE)
            if s == F:
                total = jnp.dot(place_other, remote[s, :, cols], preferred_element_type=F32)
            else:
                total = jnp.dot(
                    place_both(s, 1 - zh), both[1, :, cols], preferred_element_type=F32
                )
            total += rows[s, mx, my, :, cols].astype(F32)
            rows[s, mx, my, :, cols] = total.astype(BF16)

    def up4(i):
        return (i + 4) % 4

    def one(h, i):
        return (up4(i), my) if h == 0 else (mx, up4(i))

    def span(s):
        return EXTRA // 2 if s == X else COLS

    def g1(s, h, i, start, width):
        x, y = one(h, i)
        if s == X:
            return extra.at[x, y, :, pl.ds(h * span(s) + start, width)]
        return rows.at[s, x, y, :, pl.ds(h * COLS + start, width)]

    def g4(s, h, j, start, width):
        cols = pl.ds(h * span(s) + start, width)
        if s == X:
            return extra.at[:, up4(j), :, cols] if h == 0 else extra.at[up4(j), :, :, cols]
        if h == 0:
            return rows.at[s, :, up4(j), :, cols]
        return rows.at[s, up4(j), :, :, cols]

    first, second = (mx, my), (my, mx)

    def dev1(h, step):
        return at(mx + step, my) if h == 0 else at(mx, my + step)

    def dev2(h, step):
        return at(mx, my + step) if h == 0 else at(mx + step, my)

    gathers = {}

    def gsend(s, h, k, ref, device):
        gathers[s, h, k] = send(ref, ref, ag_send.at[s, h, k], ag_recv.at[s, h, k], device)

    def gather1(s):
        for h in (0, 1):
            ref = g1(s, h, first[h], 0, span(s))
            gsend(s, h, 0, ref, dev1(h, 1))
            gsend(s, h, 1, ref, dev1(h, -1))

    def gather2(s):
        for h in (0, 1):
            gathers[s, h, 0].wait_recv()
            gsend(s, h, 2, g1(s, h, first[h] - 1, 0, span(s) // 2), dev1(h, 1))
            gathers[s, h, 1].wait_recv()
            gsend(s, h, 3, g1(s, h, first[h] + 1, span(s) // 2, span(s) // 2), dev1(h, -1))

    def gather3(s):
        for h in (0, 1):
            gathers[s, h, 2].wait_recv()
            gathers[s, h, 3].wait_recv()
            ref = g4(s, h, second[h], 0, span(s))
            gsend(s, h, 4, ref, dev2(h, 1))
            gsend(s, h, 5, ref, dev2(h, -1))

    def gather4(s):
        for h in (0, 1):
            gathers[s, h, 4].wait_recv()
            gsend(s, h, 6, g4(s, h, second[h] - 1, 0, span(s) // 2), dev2(h, 1))
            gathers[s, h, 5].wait_recv()
            gsend(s, h, 7, g4(s, h, second[h] + 1, span(s) // 2, span(s) // 2), dev2(h, -1))

    def gather5(s):
        for h in (0, 1):
            gathers[s, h, 6].wait_recv()
            gathers[s, h, 7].wait_recv()

    def gathered_out(s):
        for h in (0, 1):
            for k in range(8):
                gathers[s, h, k].wait_send()

    def pre_copy(s, i):
        return pltpu.make_async_remote_copy(
            src_ref=part.at[s, i],
            dst_ref=peer.at[s, i],
            send_sem=pre_send.at[s, i],
            recv_sem=pre_recv.at[s, i],
            device_id=pair,
            device_id_type=MESH,
        )

    last = (((1,), (1,)), ((), ()))
    lead = (((0,), (0,)), ((), ()))

    def turn(n):
        return (mx + 2 + n) % 4

    def partial_up(s):
        def step(n, carry):
            i = turn(n)
            block = rows[s, i].reshape(4 * BLOCK, HALF)
            for u in (0, 1):
                value = jnp.dot(block, wu[u], preferred_element_type=F32)
                part[s, i, :, pl.ds(u * UNITS, UNITS)] = value.astype(BF16)
            pre_copy(s, i).start()
            return carry

        lax.fori_loop(0, 4, step, 0)

    def partial_back(s):
        def step(n, carry):
            i = turn(n)
            block = rows[s, i].reshape(4 * BLOCK, HALF)
            for u in (0, 1):
                value = lax.dot_general(block, wd[u], last, preferred_element_type=F32)
                part[s, i, :, pl.ds(u * UNITS, UNITS)] = value.astype(BF16)
            pre_copy(s, i).start()
            return carry

        lax.fori_loop(0, 4, step, 0)

    def whole(s, i, u):
        here = part[s, i, :, pl.ds(u * UNITS, UNITS)].astype(F32)
        return here + peer[s, i, :, pl.ds((1 - u) * UNITS, UNITS)].astype(F32)

    def sigmoid(value):
        return 1.0 / (1.0 + jnp.exp(-value))

    def activate_back():
        def step(i, carry):
            pre_copy(B, i).wait_recv()
            pre_copy(B, i).wait_send()
            hidden, slope = [], []
            for u in (0, 1):
                pre = whole(B, i, u)
                gate = sigmoid(pre)
                hidden.append((pre * gate).astype(BF16))
                slope.append((gate * (1.0 + pre * (1.0 - gate))).astype(BF16))
            for u in (0, 1):
                peer[B, i, :, pl.ds(u * UNITS, UNITS)] = hidden[u]
                part[B, i, :, pl.ds(u * UNITS, UNITS)] = slope[u]
            return carry

        lax.fori_loop(0, 4, step, 0)

    def back_grad(i):
        pre_copy(G, i).wait_recv()
        value = []
        for u in (0, 1):
            slope = part[B, i, :, pl.ds(u * UNITS, UNITS)].astype(F32)
            value.append((whole(G, i, u) * slope).astype(BF16))
        for u in (0, 1):
            peer[G, i, :, pl.ds(u * UNITS, UNITS)] = value[u]

    def activate_fwd(i):
        pre_copy(F, i).wait_recv()
        hidden = []
        for u in (0, 1):
            pre = whole(F, i, u)
            hidden.append((pre * sigmoid(pre)).astype(BF16))
        for u in (0, 1):
            peer[F, i, :, pl.ds(u * UNITS, UNITS)] = hidden[u]

    def down_grad():
        for u, width in ((1, KEPT), (0, HALF)):
            def step(c, carry):
                cols = pl.ds(pl.multiple_of(c * WIDE, WIDE), WIDE)
                left = peer[B, :, :, pl.ds(u * UNITS, UNITS)].reshape(16 * BLOCK, UNITS)
                right = rows[G, :, :, :, cols].reshape(16 * BLOCK, WIDE)
                value = lax.dot_general(left, right, lead, preferred_element_type=F32)
                dgs[u, :, cols] = value.astype(BF16)
                return carry

            lax.fori_loop(0, width // WIDE, step, 0)

    def down_grad_extra():
        def step(c, carry):
            start = pl.multiple_of(c * WIDE, WIDE)
            left = peer[B, :, :, pl.ds(0, UNITS)].reshape(16 * BLOCK, UNITS)
            right = extra[:, :, :, pl.ds(start, WIDE)].reshape(16 * BLOCK, WIDE)
            value = lax.dot_general(left, right, lead, preferred_element_type=F32)
            dgs[1, :, pl.ds(KEPT + start, WIDE)] = value.astype(BF16)
            return carry

        lax.fori_loop(0, EXTRA // WIDE, step, 0)

    def up_grad():
        def step(c, carry):
            cols = pl.ds(pl.multiple_of(c * TILE, TILE), TILE)
            left = rows[B, :, :, :, cols].reshape(16 * BLOCK, TILE)
            for u in (0, 1):
                right = peer[G, :, :, pl.ds(u * UNITS, UNITS)].reshape(16 * BLOCK, UNITS)
                value = lax.dot_general(left, right, lead, preferred_element_type=F32)
                wu[u, cols, :] = value.astype(BF16)
            return carry

        lax.fori_loop(0, HALF // TILE, step, 0)

    def rows_out(s, activate, weights, dims):
        def column(n, carry):
            i = turn(n)
            activate(i)

            def step(c, carry):
                cols = pl.ds(pl.multiple_of(c * TILE, TILE), TILE)
                total = None
                for u in (0, 1):
                    left = peer[s, i, :, pl.ds(u * UNITS, UNITS)]
                    right = weights[u, cols, :] if dims == last else weights[u, :, cols]
                    if dims == last:
                        value = lax.dot_general(left, right, last, preferred_element_type=F32)
                    else:
                        value = jnp.dot(left, right, preferred_element_type=F32)
                    total = value if total is None else total + value
                rows[s, i, :, :, cols] = total.astype(BF16).reshape(4, BLOCK, TILE)
                return carry

            lax.fori_loop(0, HALF // TILE, step, 0)
            return carry

        lax.fori_loop(0, 1, column, 0)
        scatter1(s, 1)
        lax.fori_loop(1, 4, column, 0)
        scatter1(s, 0)

    scatters = {}

    def ssend(s, h, k, src, dst, device):
        scatters[s, h, k] = send(src, dst, rs_send.at[s - 1, h, k], rs_recv.at[s - 1, h, k], device)

    def add4(s, h, j, start, width, sources):
        cols = pl.ds(h * COLS + start, width)

        def step(i, carry):
            x, y = (i, up4(j)) if h == 0 else (up4(j), i)
            total = rows[s, x, y, :, cols].astype(F32)
            for source in sources:
                total += source[i].astype(F32)
            rows[s, x, y, :, cols] = total.astype(BF16)
            return carry

        lax.fori_loop(0, 4, step, 0)

    def sum1(s, h, i, start, width, sources):
        x, y = one(h, i)
        total = rows[s, x, y, :, pl.ds(h * COLS + start, width)].astype(F32)
        for source in sources:
            total += source[...].astype(F32)
        rows[s, x, y, :, pl.ds(h * COLS + start, width)] = total.astype(BF16)

    def scatter1(s, h):
        far = second[h] + 2
        ssend(s, h, 0, g4(s, h, far, 0, QUARTER), r1.at[s - 1, h, 0], dev2(h, 1))
        ssend(s, h, 1, g4(s, h, far, QUARTER, QUARTER), r1.at[s - 1, h, 1], dev2(h, -1))

    def scatter2(s):
        for h in (1, 0):
            scatters[s, h, 0].wait_recv()
            add4(s, h, second[h] + 1, 0, QUARTER, [r1.at[s - 1, h, 0]])
            ssend(s, h, 2, g4(s, h, second[h] + 1, 0, COLS), r2.at[s - 1, h, 0], dev2(h, 1))
            scatters[s, h, 1].wait_recv()
            add4(s, h, second[h] - 1, QUARTER, QUARTER, [r1.at[s - 1, h, 1]])
            ssend(s, h, 3, g4(s, h, second[h] - 1, 0, COLS), r2.at[s - 1, h, 1], dev2(h, -1))

    def scatter3(s):
        for h in (0, 1):
            scatters[s, h, 2].wait_recv()
            scatters[s, h, 3].wait_recv()
            add4(s, h, second[h], 0, COLS, [r2.at[s - 1, h, 0], r2.at[s - 1, h, 1]])
            far = first[h] + 2
            ssend(s, h, 4, g1(s, h, far, 0, QUARTER), r3.at[s - 1, h, 0], dev1(h, 1))
            ssend(s, h, 5, g1(s, h, far, QUARTER, QUARTER), r3.at[s - 1, h, 1], dev1(h, -1))

    def scatter4(s):
        for h in (0, 1):
            scatters[s, h, 4].wait_recv()
            sum1(s, h, first[h] + 1, 0, QUARTER, [r3.at[s - 1, h, 0]])
            ssend(s, h, 6, g1(s, h, first[h] + 1, 0, COLS), r4.at[s - 1, h, 0], dev1(h, 1))
            scatters[s, h, 5].wait_recv()
            sum1(s, h, first[h] - 1, QUARTER, QUARTER, [r3.at[s - 1, h, 1]])
            ssend(s, h, 7, g1(s, h, first[h] - 1, 0, COLS), r4.at[s - 1, h, 1], dev1(h, -1))

    def scatter5(s, mine_ref, other_ref):
        for h in (0, 1):
            scatters[s, h, 6].wait_recv()
            scatters[s, h, 7].wait_recv()
            sum1(s, h, first[h], 0, COLS, [r4.at[s - 1, h, 0], r4.at[s - 1, h, 1]])
        for c in range(0, HALF, TILE):
            cols = pl.ds(c, TILE)
            block = rows[s, mx, my, :, cols]
            mine_ref[:, cols] = lax.dot_general(
                place_mine, block, lead, preferred_element_type=F32
            ).astype(BF16)
            other_ref[:, cols] = lax.dot_general(
                place_other, block, lead, preferred_element_type=F32
            ).astype(BF16)

    pack(F, upper, order_f, active_f, weight_f)
    fetched[G] = fetch(xg_ref, upper, 0)
    pack(B, lower, order_b, active_b, weight_b)
    wu_in.append(up_part(1))
    wu_own = keep(up_ref.at[mine], wu.at[0], 4)
    wd_own = keep(down_ref.at[:, mine], wd.at[0], 5)
    pack(G, upper, order_b, active_b, weight_b)
    wu_in.append(up_part(2))
    wu_in.append(up_part(3))
    fill(F)
    gather1(F)
    gather2(F)
    gather3(F)
    wd_in = zsend(down_ref.at[:, other], wd.at[1], 4)
    fill(B)
    gather1(B)
    gather2(B)
    gather4(F)
    gather3(B)
    fill(G)
    gather1(G)
    gather5(F)
    fill_extra()
    for copy in wu_in:
        copy.wait_recv()
    wu_own.wait()
    partial_up(F)
    gather4(B)
    gather2(G)
    gather3(G)
    gather5(B)
    partial_up(B)
    gather4(G)
    gathered_out(F)
    wd_in.wait_recv()
    wd_own.wait()
    rows_out(F, activate_fwd, wd, None)
    gather5(G)
    partial_back(G)
    scatter2(F)
    fin = zsend(xf_ref, fin_ref, 10, (after, me))
    activate_back()
    gather1(X)
    down_grad()
    gather2(X)
    kept = pl.ds(pl.multiple_of(zh * HALF, HALF), KEPT)
    dg_out = zsend(dgs.at[1, :, pl.ds(0, KEPT)], dg_ref.at[:, kept], 5)
    dg_own = keep(dgs.at[0], dg_ref.at[:, mine], 6)
    gathered_out(G)
    scatter3(F)
    told = zsend(info, info_ref, 3, (after, me))
    rows_out(G, back_grad, wu, last)
    gather3(X)
    up_grad()
    ug_out = zsend(wu.at[1], ug_ref.at[mine], 6)
    ug_own = keep(wu.at[0], ug_ref.at[mine], 7)
    scatter2(G)
    scatter4(F)
    gather4(X)
    token[G].wait_send()
    token[F].wait_send()
    token[X].wait_send()
    scatter5(F, local.at[2], remote.at[0])
    near_out = zsend(local.at[2], fout_ref.at[zh], 8, (after, me))
    far_out = zsend(remote.at[0], fout_ref.at[zh], 9, (after, mate))
    scatter3(G)
    scatter4(G)
    scatter5(G, local.at[0], local.at[1])
    row_own = keep(local.at[0], rout_ref.at[zh], 8)
    row_out = zsend(local.at[1], rout_ref.at[zh], 7)
    gather5(X)
    down_grad_extra()
    far = pl.ds(pl.multiple_of((1 - zh) * HALF + KEPT, WIDE), EXTRA)
    dg_far = keep(dgs.at[1, :, pl.ds(KEPT, EXTRA)], dg_ref.at[:, far], 9)

    for copy in (dg_own, dg_far, ug_own, row_own):
        copy.wait()
    for copy in (dg_out, ug_out, row_out, near_out, far_out, fin, told):
        copy.wait()
    for copy in wu_in:
        copy.wait_send()
    wd_in.wait_send()
    gathered_out(B)
    gathered_out(X)
    for s in (G, F):
        for h in (0, 1):
            for k in range(8):
                scatters[s, h, k].wait_send()

    def done(n, carry):
        pre_copy(n // 4, n % 4).wait_send()
        return carry

    lax.fori_loop(4, 12, done, 0)


def relay(plans, xb, xg, xf, upper, lower):
    hbm = pl.BlockSpec(memory_space=pl.ANY)
    shapes = [
        jax.ShapeDtypeStruct(xf.shape, BF16),
        jax.ShapeDtypeStruct((2, SLOTS, HALF), BF16),
        jax.ShapeDtypeStruct((2, SLOTS, HALF), BF16),
        jax.ShapeDtypeStruct(upper.shape, BF16),
        jax.ShapeDtypeStruct(lower.shape, BF16),
        jax.ShapeDtypeStruct((8, TOKENS), F32),
    ]
    dma = pltpu.SemaphoreType.DMA
    return pl.pallas_call(
        kernel,
        out_shape=shapes,
        in_specs=[pl.BlockSpec(memory_space=pltpu.VMEM)] * 4 + [hbm] * 5,
        out_specs=[hbm] * 6,
        scratch_shapes=[
            pltpu.VMEM((8, TOKENS), F32),
            pltpu.VMEM((3, 4, 4, BLOCK, HALF), BF16),
            pltpu.VMEM((4, 4, BLOCK, EXTRA), BF16),
            pltpu.VMEM((2, BLOCK, HALF), BF16),
            pltpu.VMEM((SLOTS, EXTRA), BF16),
            pltpu.VMEM((SLOTS, EXTRA), BF16),
            pltpu.VMEM((2, HALF, UNITS), BF16),
            pltpu.VMEM((2, UNITS, HALF), BF16),
            pltpu.VMEM((3, SLOTS, HALF), BF16),
            pltpu.VMEM((3, SLOTS, HALF), BF16),
            pltpu.VMEM((3, 4, 4 * BLOCK, 2 * UNITS), BF16),
            pltpu.VMEM((3, 4, 4 * BLOCK, 2 * UNITS), BF16),
            pltpu.VMEM((2, UNITS, HALF), BF16),
            pltpu.VMEM((2, 2, 2, 4, BLOCK, QUARTER), BF16),
            pltpu.VMEM((2, 2, 2, 4, BLOCK, COLS), BF16),
            pltpu.VMEM((2, 2, 2, BLOCK, QUARTER), BF16),
            pltpu.VMEM((2, 2, 2, BLOCK, COLS), BF16),
            dma((4, 2, 8)),
            dma((4, 2, 8)),
            dma((2, 2, 8)),
            dma((2, 2, 8)),
            dma((3, 4)),
            dma((3, 4)),
            dma((16,)),
            dma((16,)),
            dma((10,)),
        ],
        compiler_params=pltpu.CompilerParams(
            collective_id=0, has_side_effects=True, vmem_limit_bytes=64 * 1024 * 1024
        ),
        cost_estimate=pl.CostEstimate(
            flops=28_000_000_000, bytes_accessed=40_000_000, transcendentals=2_000_000
        ),
        name="relay",
    )(*plans, xb, xg, xf, upper, lower)


def column(line):
    down = lax.broadcasted_iota(jnp.int32, (TOKENS, TOKENS), 0)
    across = lax.broadcasted_iota(jnp.int32, (TOKENS, TOKENS), 1)
    return jnp.sum(jnp.where(down == across, line, 0.0), axis=1, keepdims=True)


def finish_kernel(
    ids_ref,
    shares_ref,
    info_ref,
    xg_ref,
    fin_ref,
    fout_ref,
    rout_ref,
    ug_ref,
    dg_ref,
    next_ref,
    grad_ref,
    up_ref,
    down_ref,
    xg,
    fin,
    fout,
    rout,
    up_held,
    down_held,
    row_sem,
    sem,
):
    halves = [pl.ds(half * HALF, HALF) for half in (0, 1)]

    def copy(src, dst, index, half):
        return pltpu.make_async_copy(src, dst, row_sem.at[index, half])

    row_loads = [
        [
            copy(fout_ref.at[half], fout.at[half], 0, half),
            copy(rout_ref.at[half], rout.at[half], 1, half),
            copy(fin_ref.at[:, halves[half]], fin.at[:, halves[half]], 2, half),
            copy(xg_ref.at[:, halves[half]], xg.at[:, halves[half]], 3, half),
        ]
        for half in (0, 1)
    ]
    row_stores = [
        [
            copy(fin.at[:, halves[half]], next_ref.at[:, halves[half]], 4, half),
            copy(xg.at[:, halves[half]], grad_ref.at[:, halves[half]], 5, half),
        ]
        for half in (0, 1)
    ]
    loads, stores = [], []
    for n in range(4):
        for k, (src, held, dst) in enumerate(((ug_ref, up_held, up_ref), (dg_ref, down_held, down_ref))):
            part = pl.ds(n * (src.shape[0] // 4), src.shape[0] // 4)
            loads.append(pltpu.make_async_copy(src.at[part], held.at[part], sem.at[0, k, n]))
            stores.append(pltpu.make_async_copy(held.at[part], dst.at[part], sem.at[1, k, n]))
    for load in row_loads[0] + row_loads[1] + loads:
        load.start()
    expert = lax.axis_index("section")
    order, active, _ = route(ids_ref, shares_ref, expert)
    lead = (((0,), (0,)), ((), ()))
    place = lax.broadcasted_iota(jnp.int32, (SLOTS, TOKENS), 0).astype(F32)
    mine = jnp.where((order == place) & (active > 0.0), 1.0, 0.0).astype(BF16)
    theirs = jnp.where(info_ref[0:1, :] == place, 1.0, 0.0).astype(BF16)
    weight = column(info_ref[1:2, :])
    moves = iter(zip(loads, stores))
    for half in (0, 1):
        for load in row_loads[half]:
            load.wait()
        for c in range(0, HALF, TILE):
            here, there = pl.ds(c, TILE), pl.ds(half * HALF + c, TILE)
            spread = lax.dot_general(theirs, fout[half, :, here], lead, preferred_element_type=F32)
            fin[:, there] = (fin[:, there].astype(F32) + weight * spread).astype(BF16)
            spread = lax.dot_general(mine, rout[half, :, here], lead, preferred_element_type=F32)
            xg[:, there] = (xg[:, there].astype(F32) + spread).astype(BF16)
            load, store = next(moves)
            load.wait()
            store.start()
        for store in row_stores[half]:
            store.start()
    for store in stores + row_stores[0] + row_stores[1]:
        store.wait()


def finish(plan, info, xg, fin, fout, rout, up_grad, down_grad):
    hbm = pl.BlockSpec(memory_space=pl.ANY)
    vmem = pl.BlockSpec(memory_space=pltpu.VMEM)
    held = (xg, fin, fout, rout, up_grad, down_grad)
    return pl.pallas_call(
        finish_kernel,
        out_shape=[jax.ShapeDtypeStruct(a.shape, BF16) for a in (fin, xg, up_grad, down_grad)],
        in_specs=[vmem] * 3 + [hbm] * 6,
        out_specs=[hbm] * 4,
        scratch_shapes=[pltpu.VMEM(a.shape, BF16) for a in held]
        + [pltpu.SemaphoreType.DMA((6, 2)), pltpu.SemaphoreType.DMA((2, 2, 4))],
        compiler_params=pltpu.CompilerParams(vmem_limit_bytes=64 * 1024 * 1024),
        cost_estimate=pl.CostEstimate(
            flops=150_000_000, bytes_accessed=20_000_000, transcendentals=0
        ),
        name="finish",
    )(*plan, info, xg, fin, fout, rout, up_grad, down_grad)


def body(
    fwd_input,
    fwd_routes,
    fwd_weights,
    bwd_input,
    bwd_routes,
    bwd_weights,
    out_grad,
    up_weight,
    down_weight,
):
    plans = [fwd_routes[0].T, fwd_weights[0].T, bwd_routes[0].T, bwd_weights[0].T]
    fin, fout, rout, up_grad, down_grad, info = relay(
        plans, bwd_input[0], out_grad[0], fwd_input[0], up_weight[0], down_weight[0]
    )
    outs = finish(plans[2:], info, out_grad[0], fin, fout, rout, up_grad, down_grad)
    return tuple(out[None] for out in outs)


def solution(mesh):
    row_spec = P("section", "fsdp", None)
    in_specs = (row_spec,) * 7 + (P("section", None, "fsdp"), row_spec)
    out_specs = (row_spec, row_spec, P("section", None, "fsdp"), row_spec)
    return jax.shard_map(body, mesh=mesh, in_specs=in_specs, out_specs=out_specs, check_vma=False)
```
